128 devices in a mesh: rep: 8 (over x, z_hi), tp: 16 (over y, z_lo, core).
Axes of the slice: x: 4, y: 4, z: 4 (z_hi: 2, z_lo: 2; z = z_hi * 2 + z_lo), core: 2. Of those that a mesh axis runs over, the one named last changes fastest.
Arguments:
- token_ids: int32 [32, 4], replicated, may hold values from 0 to 76031
- cache_len: int32 [32], P('rep'), may hold values from 1 to 8192, as said below
- embed_table: bfloat16 [76032, 5120], P('rep', 'tp'), may hold values from -400 to 400
- norm_gain: bfloat16 [5120], P('tp'), may hold values from 0.099609375 to 1.8984375
- old_qkv: bfloat16 [5120, 7168], P('tp'), may hold values from -0.078125 to 0.078125
- old_out: bfloat16 [5120, 5120], P(None, 'tp'), may hold values from -0.078125 to 0.078125
- new_qkv: bfloat16 [5120, 7168], P(('tp', 'rep')), may hold values from -0.078125 to 0.078125
- new_out: bfloat16 [5120, 5120], P(None, ('tp', 'rep')), may hold values from -0.078125 to 0.078125
- kv_cache: bfloat16 [32, 8192, 2048], P('rep', 'tp'), may hold values from -400 to 400
Outputs:
- attended: bfloat16 [32, 4, 5120], P('rep', None, 'tp')
The draws below stay inside these ranges and needn't reach their ends.
Inputs may be any that keep to these rules, and one draw needn't show every extreme that they name: `cache_len`: some row's length is 8192.
All inputs are finite; a program needn't handle non-finite values.
Results may differ from the reference program's by a relative error of at most 0.009.
The reference program's roundings to bfloat16 on the way count: a program that leaves them out, or rounds other values in their place, can miss the bound.
Values may be sent and summed in bfloat16 or wider, within the bound.
No kernel may reach another device: no remote copies, remote signals or barrier semaphores. Data moves between devices by JAX's collectives and lax.ppermute only.
A program may use at most 128 MiB of HBM per device.

```python
import math
import jax
import jax.numpy as jnp
import numpy as np
from jax import lax

D = 5120
HEADS = 40
KV_HEADS = 8
HEAD_DIM = 128
VOCAB = 76032
ROWS = 4
STEPS = 4
OLD_STEPS = 2
ROWS_ALL = 32
CACHE = 8192
QKV = 7168
N_REP = 8


def draw_cache_len(key, part):
    key = jax.random.fold_in(key, 11)
    first_key, second_key = jax.random.split(key)
    lengths = jax.random.randint(first_key, (ROWS_ALL,), 1, CACHE + 1)
    chosen = jax.random.randint(second_key, (), 0, ROWS_ALL)
    return jnp.where(jnp.arange(ROWS_ALL) == chosen, CACHE, lengths).astype(jnp.int32)


def draw_embed_table(key, part):
    key = jax.random.fold_in(key, 13)
    base_key, row_key = jax.random.split(key, 2)
    row_scale = jnp.exp(jax.random.uniform(row_key, (VOCAB, 1), jnp.float32) * math.log(10.0))
    ramp = jnp.arange(D, dtype=jnp.float32) / (D - 1)
    column_scale = jnp.exp(ramp * math.log(3.0))
    values = jnp.clip(jax.random.normal(base_key, (VOCAB, D), jnp.float32), -5.0, 5.0)
    return (values * row_scale * column_scale[None, :]).astype(jnp.bfloat16)


def draw_kv_cache(key, part):
    key = jax.random.fold_in(key, 17)
    base_key = jax.random.fold_in(key, 0)
    width = 2 * KV_HEADS * HEAD_DIM
    values = jnp.clip(jax.random.normal(base_key, (ROWS_ALL, CACHE, width), jnp.float32), -5.0, 5.0)
    return values.astype(jnp.bfloat16)


def plant(values, stream_key, least, largest):
    extent = values.shape
    place = [jax.random.randint(jax.random.fold_in(stream_key, axis), (), 0, extent[axis]) for axis in range(len(extent))]
    values = values.at[tuple(place)].set(least)
    longest = extent.index(max(extent))
    place[longest] = (place[longest] + 1) % extent[longest]
    return values.at[tuple(place)].set(largest)


def steps_of(key, shape, cuts, least, high):
    gain = 1.0
    for dim, shards_of in cuts:
        heights = jax.random.uniform(jax.random.fold_in(jax.random.fold_in(key, 6), dim), (shards_of,), jnp.float32, least / len(cuts), high / len(cuts))
        gain = gain * jnp.repeat(jnp.exp(heights), shape[dim] // shards_of).reshape((-1,) + (1,) * (len(shape) - 1 - dim))
    return gain


def ranked_wide(own_key, extent, number_of, slope):
    loads = [min(1 << octave, number_of + 1 - (1 << octave)) * (1 << 20) // math.isqrt((1 << octave) ** slope) + 1 for octave in range((number_of + 1).bit_length()) if 1 << octave <= number_of]
    deviation = 1 + sum(loads) // (1 << 30)
    listing = np.cumsum(np.array([max(1, weight // deviation) for weight in loads]))
    lot = jax.random.randint(jax.random.fold_in(own_key, 1), extent, 0, int(listing[len(loads) - 1]))
    start = jnp.left_shift(1, jnp.searchsorted(jnp.asarray(listing, jnp.int32), lot, side="right").astype(jnp.int32))
    rank = start - 1 + jax.random.randint(jax.random.fold_in(own_key, 4), extent, 0, 1 << 30) % jnp.minimum(start, number_of + 1 - start)
    return jax.random.permutation(jax.random.fold_in(own_key, 2), number_of)[rank].astype(jnp.int32)


def bell_draw(own_key, extent, deviation, limit, cuts=(), kind=jnp.bfloat16):
    array = jax.random.normal(own_key, extent, jnp.float32) * deviation
    if len(cuts) > 0:
        array = steps_of(own_key, extent, cuts, -0.22, 0.18) * array
    return jnp.clip(array, min=-limit, max=limit).astype(kind)


def setup_inputs(seed: int = 0) -> dict:
    seeds = jax.random.split(jax.random.key(seed), 10)
    return {
        "token_ids": plant(ranked_wide(seeds[0], (ROWS_ALL, STEPS), VOCAB, 2), jax.random.fold_in(seeds[0], 3), 0, VOCAB - 1).astype(jnp.int32),
        "cache_len": draw_cache_len(jax.random.fold_in(seeds[9], 71), 0),
        "embed_table": draw_embed_table(jax.random.fold_in(seeds[9], 71), 0),
        "norm_gain": jnp.clip(1.0 + 0.18 * jax.random.normal(seeds[3], (D,), jnp.float32), 0.099609375, 1.8984375).astype(jnp.bfloat16),
        "old_qkv": bell_draw(seeds[4], (D, QKV), D ** -0.5, 0.078125, ((0, 16),)),
        "old_out": bell_draw(seeds[5], (HEADS * HEAD_DIM, D), (HEADS * HEAD_DIM) ** -0.5, 0.078125, ((1, 16),)),
        "new_qkv": bell_draw(seeds[6], (D, QKV), D ** -0.5, 0.078125, ((0, 128),)),
        "new_out": bell_draw(seeds[7], (HEADS * HEAD_DIM, D), (HEADS * HEAD_DIM) ** -0.5, 0.078125, ((1, 128),)),
        "kv_cache": draw_kv_cache(jax.random.fold_in(seeds[9], 71), 0),
    }


NORM_EPSILON = 1e-06
ROPE_BASE = 1000000.0
MASK_VALUE = -1e+30

def rotate(tensor, positions):
    half_dim = tensor.shape[-1] // 2
    inverse_freq = ROPE_BASE ** (-jnp.arange(half_dim, dtype=jnp.float32) * 2.0 / tensor.shape[-1])
    angles = positions.astype(jnp.float32)[:, None] * inverse_freq[None, :]
    cosine = jnp.cos(angles)[:, None, :]
    sine_part = jnp.sin(angles)[:, None, :]
    front_half = tensor[..., :half_dim]
    back_half = tensor[..., half_dim:]
    return jnp.concatenate([front_half * cosine - back_half * sine_part, back_half * cosine + front_half * sine_part], axis=-1)

def finish(summed, squares, positions):
    query_width = HEADS * HEAD_DIM
    kv_width = KV_HEADS * HEAD_DIM
    root_mean = jnp.sqrt(squares / D + NORM_EPSILON)
    normed = summed / root_mean[:, None]
    query_part = rotate(normed[:, :query_width].reshape(-1, HEADS, HEAD_DIM), positions).reshape(-1, query_width)
    key_part = rotate(normed[:, query_width:query_width + kv_width].reshape(-1, KV_HEADS, HEAD_DIM), positions).reshape(-1, kv_width)
    return jnp.concatenate([query_part, key_part, normed[:, query_width + kv_width:]], axis=1).astype(jnp.bfloat16)

def reference(token_ids, cache_len, embed_table, norm_gain, old_qkv, old_out, new_qkv, new_out, kv_cache):
    query_width = HEADS * HEAD_DIM
    kv_width = KV_HEADS * HEAD_DIM
    group_size = HEADS // KV_HEADS
    later = STEPS - OLD_STEPS
    score_scale = 1.0 / HEAD_DIM ** 0.5

    def replica_block(pieces):
        token_rows, lengths, cache_rows = pieces
        embedded = jnp.take(embed_table, token_rows, axis=0)
        embedded_wide = embedded.astype(jnp.float32)
        squares = lax.optimization_barrier(jnp.sum(embedded_wide * embedded_wide, axis=-1))
        scaled = (embedded_wide * norm_gain.astype(jnp.float32)).astype(jnp.bfloat16)
        early_sum = jnp.dot(scaled[:, :OLD_STEPS].reshape(-1, D), old_qkv, preferred_element_type=jnp.float32).reshape(ROWS, OLD_STEPS, QKV)
        late_sum = jnp.dot(scaled[:, OLD_STEPS:].reshape(-1, D), new_qkv, preferred_element_type=jnp.float32).reshape(ROWS, later, QKV)
        summed = jnp.concatenate([early_sum, late_sum], axis=1)
        positions = lengths[:, None] + jnp.arange(STEPS, dtype=jnp.int32)[None, :]
        projected = finish(summed.reshape(-1, QKV), squares.reshape(-1), positions.reshape(-1)).reshape(ROWS, STEPS, QKV)
        queries = projected[..., :query_width].reshape(ROWS, STEPS, KV_HEADS, group_size, HEAD_DIM).astype(jnp.float32)
        keys_new = projected[..., query_width:query_width + kv_width].reshape(ROWS, STEPS, KV_HEADS, HEAD_DIM).astype(jnp.float32)
        values_new = projected[..., query_width + kv_width:].reshape(ROWS, STEPS, KV_HEADS, HEAD_DIM).astype(jnp.float32)
        keys_cache = cache_rows[..., :kv_width].reshape(ROWS, CACHE, KV_HEADS, HEAD_DIM).astype(jnp.float32)
        values_cache = cache_rows[..., kv_width:].reshape(ROWS, CACHE, KV_HEADS, HEAD_DIM).astype(jnp.float32)
        scores_cache = jnp.einsum('rgkhd,rpkd->rgkhp', queries, keys_cache) * score_scale
        valid_mask = jnp.arange(CACHE, dtype=jnp.int32)[None, :] < lengths[:, None]
        scores_cache = jnp.where(valid_mask[:, None, None, None, :], scores_cache, MASK_VALUE)
        scores_new = jnp.einsum('rgkhd,rjkd->rgkhj', queries, keys_new) * score_scale
        causal = jnp.arange(STEPS, dtype=jnp.int32)[None, :] <= jnp.arange(STEPS, dtype=jnp.int32)[:, None]
        scores_new = jnp.where(causal[None, :, None, None, :], scores_new, MASK_VALUE)
        peak = jnp.maximum(lax.optimization_barrier(jnp.max(scores_cache, axis=-1)), lax.optimization_barrier(jnp.max(scores_new, axis=-1)))
        weights_cache = jnp.exp(scores_cache - peak[..., None]).astype(jnp.bfloat16).astype(jnp.float32)
        weights_new = jnp.exp(scores_new - peak[..., None]).astype(jnp.bfloat16).astype(jnp.float32)
        numerator = jnp.einsum('rgkhp,rpkd->rgkhd', weights_cache, values_cache) + jnp.einsum('rgkhj,rjkd->rgkhd', weights_new, values_new)
        denominator = lax.optimization_barrier(jnp.sum(weights_cache, axis=-1)) + lax.optimization_barrier(jnp.sum(weights_new, axis=-1))
        heads = (numerator / denominator[..., None]).astype(jnp.bfloat16).reshape(ROWS, STEPS, query_width)
        early_out = jnp.dot(heads[:, :OLD_STEPS].reshape(-1, query_width), old_out, preferred_element_type=jnp.float32).reshape(ROWS, OLD_STEPS, D)
        late_out = jnp.dot(heads[:, OLD_STEPS:].reshape(-1, query_width), new_out, preferred_element_type=jnp.float32).reshape(ROWS, later, D)
        return jnp.concatenate([early_out, late_out], axis=1).astype(jnp.bfloat16)
    result = lax.map(replica_block, (token_ids.reshape(N_REP, ROWS, STEPS), cache_len.reshape(N_REP, ROWS), kv_cache.reshape(N_REP, ROWS, CACHE, 2 * KV_HEADS * HEAD_DIM)))
    return result.reshape(ROWS_ALL, STEPS, D)
```

```python
import functools

import jax
import jax.numpy as jnp
from jax import lax
from jax.experimental import pallas as pl
from jax.experimental.pallas import tpu as pltpu
from jax.sharding import PartitionSpec as P

D = 5120
HEADS = 40
KV_HEADS = 8
HEAD_DIM = 128
GROUP = HEADS // KV_HEADS
STEPS = 4
OLD_STEPS = 2
ROWS = 4
N_X = 4
N_REP = 8
N_TP = 16
TOKENS = N_REP * ROWS * STEPS

NORM_EPSILON = 1e-06
ROPE_BASE = 1000000.0
MASK_VALUE = -1e30
SCORE_SCALE = 1.0 / HEAD_DIM**0.5

FEAT = D // N_TP
PART = FEAT // N_X
SHARD = PART // 2
LANES = 128
SLOTS = 8
HALF_HEADS = KV_HEADS // 2
HALF_ROWS = HALF_HEADS * SLOTS
BLOCK = 2 * HALF_ROWS
DESTS = N_X * 8

f32 = jnp.float32
bf16 = jnp.bfloat16
MIB = 1 << 20

VMEM = pl.BlockSpec(memory_space=pltpu.VMEM)
SMEM = pl.BlockSpec(memory_space=pltpu.SMEM)
ANY = pl.BlockSpec(memory_space=pl.ANY)


def params(mib, grid=False):
    kwargs = dict(dimension_semantics=("arbitrary",) * grid) if grid else {}
    return pltpu.CompilerParams(vmem_limit_bytes=mib * MIB, **kwargs)


def gather_kernel(ids_ref, tail_ref, table_ref, out_ref, buf, cols, sems):
    window = table_ref.shape[1]
    tail_start = window // LANES * LANES
    start = lax.axis_index("rep") * window

    def local_id(i):
        zh, el, xx = i // 64, (i // 32) % 2, (i // 8) % 4
        row, par = (i // 2) % 4, i % 2
        return ids_ref[el * 2 + par, (xx * 2 + zh) * ROWS + row] - start

    def copy(i, local):
        base = pl.multiple_of(local // LANES * LANES, LANES)
        return pltpu.make_async_copy(
            table_ref.at[:, pl.ds(base, LANES)], buf.at[i], sems.at[i]
        )

    def begin(i, carry):
        local = local_id(i)

        @pl.when((local >= 0) & (local < tail_start))
        def _():
            copy(i, local).start()

        return carry

    lax.fori_loop(0, TOKENS, begin, 0, unroll=8)
    cols[...] = jnp.zeros_like(cols)
    lane = lax.broadcasted_iota(jnp.int32, (FEAT, LANES), 1)

    def place(i, local, block):
        shift = lax.rem(i - lax.rem(local, LANES) + LANES, LANES)
        moved = pltpu.roll(block.astype(f32), shift, 1)
        cols[...] = jnp.where(lane == i, moved, cols[...])

    def end(i, carry):
        local = local_id(i)

        @pl.when((local >= 0) & (local < tail_start))
        def _():
            copy(i, local).wait()
            place(i, local, buf[i])

        @pl.when((local >= tail_start) & (local < window))
        def _():
            place(i, local, tail_ref[...])

        return carry

    lax.fori_loop(0, TOKENS, end, 0)
    out_ref[...] = jnp.zeros_like(out_ref)
    for xx in range(N_X):
        rows = cols[xx * PART : (xx + 1) * PART, :].T.astype(bf16)
        for zh in range(2):
            out_ref[xx * 2 + zh, :, :PART] = rows[zh * 64 : (zh + 1) * 64]


def gather_rows(token_ids, embed_table):
    table = embed_table.T
    tail = table.shape[1] // LANES
    return pl.pallas_call(
        gather_kernel,
        grid=(1,),
        in_specs=[
            pl.BlockSpec(memory_space=pltpu.SMEM),
            pl.BlockSpec((FEAT, LANES), lambda i: (0, tail)),
            ANY,
        ],
        out_specs=pl.BlockSpec((N_REP, 64, LANES), lambda i: (0, 0, 0)),
        out_shape=jax.ShapeDtypeStruct((N_REP, 64, LANES), bf16),
        scratch_shapes=[
            pltpu.VMEM((TOKENS, FEAT, LANES), bf16),
            pltpu.VMEM((FEAT, LANES), f32),
            pltpu.SemaphoreType.DMA((TOKENS,)),
        ],
        compiler_params=params(24),
        name="gather_rows",
    )(token_ids.T, table, table)


def project_kernel(x_ref, gain_ref, new_ref, other_ref, old_ref, keep_ref, send_ref, old, sem):
    rep, tp = lax.axis_index("rep"), lax.axis_index("tp")
    xx, zh, core = rep // 2, rep % 2, tp % 2
    copy = pltpu.make_async_copy(
        old_ref.at[pl.ds(pl.multiple_of(xx * PART, 16), PART), :], old, sem
    )
    copy.start()
    embedded = jnp.sum(x_ref[...].astype(f32), axis=0)
    squares = jnp.sum(embedded * embedded, axis=1, keepdims=True)
    wide = gain_ref[...].astype(f32)
    gain = jnp.zeros((1, PART), f32)
    for i in range(N_X):
        gain = gain + jnp.where(xx == i, wide[:, i * PART : (i + 1) * PART], 0.0)
    scaled = (embedded[:, :PART] * gain).astype(bf16)
    early, late = scaled[:DESTS], scaled[DESTS:]
    first, second = late[:, :SHARD], late[:, SHARD:]
    late_own = jnp.where(zh == 0, first, second)
    late_other = jnp.where(zh == 0, second, first)
    copy.wait()
    for out_ref, half in ((keep_ref, core), (send_ref, 1 - core)):
        for j in range(HALF_HEADS):
            head = half * HALF_HEADS + j
            starts = (
                (head * (GROUP * HEAD_DIM), GROUP * HEAD_DIM, 0),
                (HEADS * HEAD_DIM + head * HEAD_DIM, HEAD_DIM, GROUP),
                ((HEADS + KV_HEADS) * HEAD_DIM + head * HEAD_DIM, HEAD_DIM, GROUP + 1),
            )
            for start, width, slot in starts:
                columns = pl.ds(pl.multiple_of(start, HEAD_DIM), width)
                sums = (
                    jnp.dot(early, old[:, columns], preferred_element_type=f32),
                    jnp.dot(late_own, new_ref[:, columns], preferred_element_type=f32)
                    + jnp.dot(late_other, other_ref[:, columns], preferred_element_type=f32),
                )
                for el in range(2):
                    for g in range(width // HEAD_DIM):
                        at = el * HALF_ROWS + j * SLOTS + slot + g
                        out_ref[pl.ds(at, DESTS, stride=BLOCK), :] = sums[el][
                            :, g * HEAD_DIM : (g + 1) * HEAD_DIM
                        ]
            for el in range(2):
                at = el * HALF_ROWS + j * SLOTS + SLOTS - 1
                out_ref[pl.ds(at, DESTS, stride=BLOCK), :] = jnp.broadcast_to(
                    squares[el * DESTS : (el + 1) * DESTS], (DESTS, LANES)
                )


def project(received, norm_gain, new_qkv, other_qkv, old_qkv):
    width = old_qkv.shape[1]
    out = jax.ShapeDtypeStruct((DESTS * BLOCK, LANES), f32)
    return pl.pallas_call(
        project_kernel,
        in_specs=[VMEM, VMEM, VMEM, VMEM, ANY],
        out_specs=[VMEM, VMEM],
        out_shape=[out, out],
        scratch_shapes=[pltpu.VMEM((PART, width), bf16), pltpu.SemaphoreType.DMA],
        compiler_params=params(24),
        name="project",
    )(received, norm_gain.reshape(1, FEAT), new_qkv, other_qkv, old_qkv)


def finish_kernel(x_ref, cos_ref, sin_ref, out_ref):
    summed = jnp.sum(x_ref[...], axis=0).reshape(2, HALF_HEADS, SLOTS, LANES)
    squares = summed[:, :, SLOTS - 1 :, :]
    normed = summed / jnp.sqrt(squares / D + NORM_EPSILON)
    swapped = pltpu.roll(normed.reshape(BLOCK, LANES), HEAD_DIM // 2, 1).reshape(normed.shape)
    rotated = normed * cos_ref[...].reshape(2, 1, 1, LANES) + swapped * sin_ref[...].reshape(
        2, 1, 1, LANES
    )
    slot = lax.broadcasted_iota(jnp.int32, normed.shape, 2)
    result = jnp.where(slot <= GROUP, rotated, jnp.where(slot == GROUP + 1, normed, 0.0))
    out_ref[...] = jnp.broadcast_to(
        result.reshape(1, BLOCK, LANES).astype(bf16), out_ref.shape
    )


def finish(received, cosine, sine):
    return pl.pallas_call(
        finish_kernel,
        in_specs=[VMEM, VMEM, VMEM],
        out_specs=VMEM,
        out_shape=jax.ShapeDtypeStruct((N_TP, BLOCK, LANES), bf16),
        compiler_params=params(16),
        name="finish",
    )(received, cosine, sine)


def attend_kernel(len_ref, q_ref, k_ref, v_ref, out_ref, q_wide, out_wide):
    row, half = pl.program_id(0), pl.program_id(1)
    tp = lax.axis_index("tp")
    chunk = k_ref.shape[1]

    @pl.when((row == 0) & (half == 0))
    def _():
        q_wide[...] = q_ref[...].reshape(q_wide.shape).astype(f32)

    valid = len_ref[row] - tp * chunk
    count = STEPS * SLOTS
    position = lax.broadcasted_iota(jnp.int32, (count, chunk), 1)
    cache_mask = position < valid
    from_step = lax.broadcasted_iota(jnp.int32, (count, count), 0) // SLOTS
    column = lax.broadcasted_iota(jnp.int32, (count, count), 1)
    new_mask = (column % SLOTS == GROUP) & (column // SLOTS <= from_step) & (tp == 0)
    slot = lax.broadcasted_iota(jnp.int32, (STEPS, SLOTS, LANES), 1)
    diagonal = slot == lax.broadcasted_iota(jnp.int32, (STEPS, SLOTS, LANES), 2)
    for j in range(HALF_HEADS):
        at = [
            pl.multiple_of(
                ((row * 2 + s % 2) * 2 + half) * BLOCK + (s // 2) * HALF_ROWS + j * SLOTS, SLOTS
            )
            for s in range(STEPS)
        ]
        wide = jnp.concatenate([q_wide[pl.ds(a, SLOTS), :] for a in at], axis=0)
        queries = wide.astype(bf16)
        shifted = pltpu.roll(wide, count - 1, 0).astype(bf16)
        columns = slice(j * HEAD_DIM, (j + 1) * HEAD_DIM)
        contract_last = (((1,), (1,)), ((), ()))
        scores = lax.dot_general(
            queries, k_ref[0, :, columns], contract_last, preferred_element_type=f32
        )
        scores = jnp.where(cache_mask, scores * SCORE_SCALE, MASK_VALUE)
        scores_new = lax.dot_general(
            queries, queries, contract_last, preferred_element_type=f32
        )
        scores_new = jnp.where(new_mask, scores_new * SCORE_SCALE, MASK_VALUE)
        peak = jnp.maximum(
            jnp.max(scores, axis=1, keepdims=True), jnp.max(scores_new, axis=1, keepdims=True)
        )
        weights = jnp.exp(scores - peak).astype(bf16)
        weights_new = jnp.exp(scores_new - peak).astype(bf16)
        total = jnp.sum(weights.astype(f32), axis=1, keepdims=True) + jnp.sum(
            weights_new.astype(f32), axis=1, keepdims=True
        )
        numerator = jnp.dot(
            weights, v_ref[0, :, columns], preferred_element_type=f32
        ) + jnp.dot(weights_new, shifted, preferred_element_type=f32)
        part = (numerator / total).reshape(STEPS, SLOTS, LANES)
        log_total = (peak + jnp.log(total)).reshape(STEPS, SLOTS, 1)
        log_row = jnp.sum(jnp.where(diagonal, log_total, 0.0), axis=1, keepdims=True)
        high = log_row.astype(bf16).astype(f32)
        middle = (log_row - high).astype(bf16).astype(f32)
        low = log_row - high - middle
        part = jnp.where(
            slot < GROUP,
            part,
            jnp.where(slot == GROUP, high, jnp.where(slot == GROUP + 1, middle, low)),
        )
        for s in range(STEPS):
            out_wide[pl.ds(at[s], SLOTS), :] = part[s]

    @pl.when((row == ROWS - 1) & (half == 1))
    def _():
        out_ref[...] = out_wide[...].astype(bf16).reshape(out_ref.shape)


def attend(cache_len, gathered, kv_cache):
    chunk = kv_cache.shape[1]
    width = HALF_HEADS * HEAD_DIM
    whole = pl.BlockSpec((N_TP, BLOCK, LANES), lambda r, h: (0, 0, 0))
    return pl.pallas_call(
        attend_kernel,
        grid=(ROWS, 2),
        in_specs=[
            pl.BlockSpec(memory_space=pltpu.SMEM),
            whole,
            pl.BlockSpec((1, chunk, width), lambda r, h: (r, 0, h)),
            pl.BlockSpec((1, chunk, width), lambda r, h: (r, 0, 2 + h)),
        ],
        out_specs=whole,
        out_shape=jax.ShapeDtypeStruct((N_TP, BLOCK, LANES), bf16),
        scratch_shapes=[
            pltpu.VMEM((N_TP * BLOCK, LANES), f32),
            pltpu.VMEM((N_TP * BLOCK, LANES), f32),
        ],
        compiler_params=params(24, 2),
        name="attend",
    )(cache_len, gathered, kv_cache, kv_cache)


def merge_kernel(x_ref, out_ref):
    x = x_ref[...].astype(f32).reshape(N_TP, 2 * HALF_HEADS, SLOTS, LANES)
    log_row = jnp.sum(x[:, :, GROUP:, :], axis=2, keepdims=True)
    slot = lax.broadcasted_iota(jnp.int32, x.shape, 2)
    lane = lax.broadcasted_iota(jnp.int32, x.shape, 3)
    log_total = jnp.sum(jnp.where(slot == lane, log_row, 0.0), axis=3, keepdims=True)
    share = jnp.exp(log_total - jnp.max(log_total, axis=0, keepdims=True))
    heads = jnp.sum(share * x, axis=0) / jnp.sum(share, axis=0)
    out_ref[...] = jnp.broadcast_to(
        heads.reshape(1, BLOCK, LANES).astype(bf16), out_ref.shape
    )


def merge(received):
    return pl.pallas_call(
        merge_kernel,
        in_specs=[VMEM],
        out_specs=VMEM,
        out_shape=jax.ShapeDtypeStruct((N_TP, BLOCK, LANES), bf16),
        compiler_params=params(16),
        name="merge",
    )(received)


def output_kernel(x_ref, old_ref, new_ref, out_ref, wide, heads, early_sum, late_sum):
    step = pl.program_id(0)
    half = N_TP // 2

    @pl.when(step == 0)
    def _():
        wide[...] = x_ref[...].reshape(wide.shape).astype(f32)
        early_sum[...] = jnp.zeros_like(early_sum)
        late_sum[...] = jnp.zeros_like(late_sum)
        for h in range(HEADS):
            core, j, g = h // (HEADS // 2), h // GROUP % HALF_HEADS, h % GROUP
            at = core * BLOCK + j * SLOTS + g
            rows = [
                wide[pl.ds(at + el * HALF_ROWS, half, stride=2 * BLOCK), :] for el in range(2)
            ]
            both = jnp.concatenate(rows, axis=0).astype(bf16)
            per_step = HEADS // heads.shape[0]
            heads[h // per_step, :, h % per_step * HEAD_DIM : (h % per_step + 1) * HEAD_DIM] = both

    contract_last = (((1,), (1,)), ((), ()))
    both = heads[step]
    early_sum[...] += lax.dot_general(
        both[:half], old_ref[...], contract_last, preferred_element_type=f32
    )
    late_sum[...] += lax.dot_general(
        both[half:], new_ref[...], contract_last, preferred_element_type=f32
    )

    @pl.when(step == pl.num_programs(0) - 1)
    def _():
        for r in range(ROWS):
            for el, total in enumerate((early_sum, late_sum)):
                out_ref[r, el * 2 : el * 2 + 2, :] = total[r * 2 : r * 2 + 2, :].astype(bf16)


def output(gathered, old_out, fresh_out):
    blocks = 4
    depth = D // blocks
    return pl.pallas_call(
        output_kernel,
        grid=(blocks,),
        in_specs=[
            pl.BlockSpec((N_TP, BLOCK, LANES), lambda i: (0, 0, 0)),
            pl.BlockSpec((FEAT, depth), lambda i: (0, i)),
            pl.BlockSpec((FEAT, depth), lambda i: (0, i)),
        ],
        out_specs=pl.BlockSpec((ROWS, STEPS, FEAT), lambda i: (0, 0, 0)),
        out_shape=jax.ShapeDtypeStruct((ROWS, STEPS, FEAT), bf16),
        scratch_shapes=[
            pltpu.VMEM((N_TP * BLOCK, LANES), f32),
            pltpu.VMEM((blocks, N_TP, depth), bf16),
            pltpu.VMEM((N_TP // 2, FEAT), f32),
            pltpu.VMEM((N_TP // 2, FEAT), f32),
        ],
        compiler_params=params(24, 1),
        name="output",
    )(gathered, old_out.T, fresh_out)


def rotation(cache_len):
    row = lax.axis_index("tp") // 4
    parity = lax.axis_index("tp") // 2 % 2
    half_dim = HEAD_DIM // 2
    inverse_freq = ROPE_BASE ** (-jnp.arange(half_dim, dtype=f32) * 2.0 / HEAD_DIM)
    positions = cache_len[row] + parity + 2 * jnp.arange(2, dtype=jnp.int32)
    angles = positions.astype(f32)[:, None] * inverse_freq[None, :]
    cosine, sine = jnp.cos(angles), jnp.sin(angles)
    return (
        jnp.concatenate([cosine, cosine], axis=1),
        jnp.concatenate([-sine, sine], axis=1),
    )


def body(
    token_ids, cache_len, embed_table, norm_gain, old_qkv, old_out, new_qkv, new_out, kv_cache
):
    fresh_out = lax.all_gather(new_out.T, "rep", axis=0, tiled=True)
    other_qkv = lax.ppermute(new_qkv, "rep", [(r, r ^ 1) for r in range(N_REP)])
    cosine, sine = rotation(cache_len)
    rows = gather_rows(token_ids, embed_table)
    rows = lax.all_to_all(rows, "rep", 0, 0)
    keep, send = project(rows, norm_gain, new_qkv, other_qkv, old_qkv)
    arrived = lax.ppermute(send, "tp", [(t, t ^ 1) for t in range(N_TP)])
    summed = (keep + arrived).reshape(DESTS, BLOCK, LANES)
    groups = [
        [(x * 2 + zh) * N_TP + k * 2 + core for x in range(N_X) for k in range(8)]
        for zh in range(2)
        for core in range(2)
    ]
    partials = lax.all_to_all(summed, ("rep", "tp"), 0, 0, axis_index_groups=groups)
    projected = lax.all_to_all(finish(partials, cosine, sine), "tp", 0, 0)
    parts = lax.all_to_all(attend(cache_len, projected, kv_cache), "tp", 0, 0)
    heads = lax.all_to_all(merge(parts), "tp", 0, 0)
    return output(heads, old_out, fresh_out)


def solution(mesh):
    in_specs = (
        P(),
        P("rep"),
        P("rep", "tp"),
        P("tp"),
        P("tp", None),
        P(None, "tp"),
        P(("tp", "rep"), None),
        P(None, ("tp", "rep")),
        P("rep", "tp", None),
    )
    out_specs = P("rep", None, "tp")
    return jax.shard_map(body, mesh=mesh, in_specs=in_specs, out_specs=out_specs, check_vma=False)
```

```python
import functools

import jax
import jax.numpy as jnp
from jax import lax
from jax.experimental import pallas as pl
from jax.experimental.pallas import tpu as pltpu
from jax.sharding import PartitionSpec as P

D = 5120
HEADS = 40
KV_HEADS = 8
HEAD_DIM = 128
GROUP = HEADS // KV_HEADS
STEPS = 4
OLD_STEPS = 2
ROWS = 4
N_REP = 8
N_TP = 16
TOKENS = N_REP * ROWS * STEPS

NORM_EPSILON = 1e-06
ROPE_BASE = 1000000.0
MASK_VALUE = -1e30
SCORE_SCALE = 1.0 / HEAD_DIM**0.5

FEAT = D // N_TP
SHARD = FEAT // N_REP
LANES = 128
HALF_TP = N_TP // 2
N_X = 4
PART = FEAT // N_X
SLOTS = 8
USED = GROUP + 2
BLOCK = KV_HEADS * SLOTS
PER_CORE = KV_HEADS // 2
HALF_ROWS = PER_CORE * SLOTS
SUMS = HALF_ROWS + SLOTS
DESTS = N_X * HALF_TP
WIDE = 3 * LANES

f32 = jnp.float32
bf16 = jnp.bfloat16
MIB = 1 << 20

VMEM = pl.BlockSpec(memory_space=pltpu.VMEM)
SMEM = pl.BlockSpec(memory_space=pltpu.SMEM)
ANY = pl.BlockSpec(memory_space=pl.ANY)


def params(mib, grid=False):
    kwargs = dict(dimension_semantics=("arbitrary",) * grid) if grid else {}
    return pltpu.CompilerParams(vmem_limit_bytes=mib * MIB, **kwargs)

def gather_kernel(ids_ref, tail_ref, table_ref, out_ref, buf, cols, found, sems):
    window = table_ref.shape[1]
    tail_start = window // LANES * LANES
    start = lax.axis_index("rep") * window

    def local_id(i):
        step = ((i >> 5) & 1) * 2 + (i & 1)
        row = ((i >> 3) & 3) * 8 + (i >> 6) * 4 + ((i >> 1) & 3)
        return ids_ref[step, row] - start

    def note(i, count):
        local = local_id(i)
        found[count] = i
        return count + ((local >= 0) & (local < window)).astype(jnp.int32)

    count = lax.fori_loop(0, TOKENS, note, jnp.int32(0), unroll=32)

    def copy(j, local):
        base = pl.multiple_of((local >> 7) << 7, LANES)
        return pltpu.make_async_copy(
            table_ref.at[:, pl.ds(base, LANES)], buf.at[j], sems.at[j]
        )

    def begin(j, carry):
        local = local_id(found[j])

        @pl.when(local < tail_start)
        def _():
            copy(j, local).start()

        return carry

    lax.fori_loop(0, count, begin, 0)
    cols[...] = jnp.zeros_like(cols)
    lane = lax.broadcasted_iota(jnp.int32, (FEAT, LANES), 1)

    def place(i, local, block):
        shift = (i - local) & (LANES - 1)
        moved = pltpu.roll(block.astype(f32), shift, 1)
        cols[:FEAT] = jnp.where(lane == i, moved, cols[:FEAT])

    def end(j, carry):
        i = found[j]
        local = local_id(i)

        @pl.when(local < tail_start)
        def _():
            copy(j, local).wait()
            place(i, local, buf[j])

        @pl.when(local >= tail_start)
        def _():
            place(i, local, tail_ref[...])

        return carry

    lax.fori_loop(0, count, end, 0)
    rows = cols[...].T
    for zh in range(2):
        early = rows[zh * 64 : zh * 64 + DESTS]
        late = rows[zh * 64 + DESTS : zh * 64 + 2 * DESTS]
        tiles = [early[:, n * LANES : (n + 1) * LANES] for n in range(WIDE // LANES)]
        for xx in range(N_X):
            part = late[:, xx * PART : (xx + 1) * PART]
            blank = jnp.zeros((DESTS, LANES - PART), f32)
            block = jnp.concatenate(tiles + [jnp.concatenate([part, blank], axis=1)], axis=0)
            out_ref[xx * 2 + zh] = block.astype(bf16)


def gather_rows(token_ids, embed_table):
    table = embed_table.T
    tail = table.shape[1] // LANES
    return pl.pallas_call(
        gather_kernel,
        grid=(1,),
        in_specs=[SMEM, pl.BlockSpec((FEAT, LANES), lambda i: (0, tail)), ANY],
        out_specs=VMEM,
        out_shape=jax.ShapeDtypeStruct((N_REP, 4 * DESTS, LANES), bf16),
        scratch_shapes=[
            pltpu.VMEM((TOKENS, FEAT, LANES), bf16),
            pltpu.VMEM((WIDE, LANES), f32),
            pltpu.SMEM((TOKENS,), jnp.int32),
            pltpu.SemaphoreType.DMA((TOKENS,)),
        ],
        compiler_params=params(60),
        name="gather_rows",
    )(token_ids.T, table, table)


def project_kernel(x_ref, gain_ref, new_ref, other_ref, old_ref, keep_ref, send_ref, old, sems):
    rep, core = lax.axis_index("rep"), lax.axis_index("tp") & 1
    xx, zh = rep >> 1, rep & 1
    copies = []
    for n, (first, width, to) in enumerate(
        (
            (0, 2 * GROUP, 0),
            (HEADS, 2, 2 * GROUP),
            (HEADS + KV_HEADS, 2, 2 * GROUP + 2),
        )
    ):
        start = pl.multiple_of((first + xx * width) * HEAD_DIM, HEAD_DIM)
        copies.append(
            pltpu.make_async_copy(
                old_ref.at[:, pl.ds(start, width * HEAD_DIM)],
                old.at[:, pl.ds(to * HEAD_DIM, width * HEAD_DIM)],
                sems.at[n],
            )
        )
        copies[-1].start()
    embedded = jnp.sum(x_ref[...].astype(f32), axis=0)
    early = jnp.concatenate(
        [embedded[n * DESTS : (n + 1) * DESTS] for n in range(WIDE // LANES)], axis=1
    )
    late = embedded[3 * DESTS :]
    squares = [
        jnp.broadcast_to(jnp.sum(e * e, axis=1, keepdims=True), (DESTS, LANES))
        for e in (late, early)
    ]
    gain = gain_ref[...].astype(f32)
    part_gain = jnp.zeros((1, PART), f32)
    for i in range(N_X):
        part_gain = part_gain + jnp.where(xx == i, gain[:, i * PART : (i + 1) * PART], 0.0)
    early = (early[:, :FEAT] * gain).astype(bf16)
    late = (late[:, :PART] * part_gain).astype(bf16)
    first, second = late[:, :SHARD], late[:, SHARD:]
    late_own = jnp.where(zh == 0, first, second)
    late_other = jnp.where(zh == 0, second, first)

    def put(out_ref, group, slot, value):
        out_ref[pl.ds(group * SLOTS + slot, DESTS, stride=SUMS), :] = value

    for out_ref, side in ((keep_ref, core), (send_ref, 1 - core)):
        for j in range(PER_CORE):
            head = j * 2 + side
            starts = (
                (head * (GROUP * HEAD_DIM), GROUP, 0),
                (HEADS * HEAD_DIM + head * HEAD_DIM, 1, GROUP),
                ((HEADS + KV_HEADS) * HEAD_DIM + head * HEAD_DIM, 1, GROUP + 1),
            )
            for start, width, slot in starts:
                columns = pl.ds(pl.multiple_of(start, HEAD_DIM), width * HEAD_DIM)
                sums = jnp.dot(
                    late_own, new_ref[:, columns], preferred_element_type=f32
                ) + jnp.dot(late_other, other_ref[:, columns], preferred_element_type=f32)
                for g in range(width):
                    put(out_ref, j, slot + g, sums[:, g * HEAD_DIM : (g + 1) * HEAD_DIM])
            put(out_ref, j, SLOTS - 1, squares[0])
    for copy in copies:
        copy.wait()
    sums = jnp.dot(early, old[...], preferred_element_type=f32)
    for slot in range(USED):
        at = (slot, slot + GROUP) if slot < GROUP else (slot * 2, slot * 2 + 1)
        both = [sums[:, a * HEAD_DIM : (a + 1) * HEAD_DIM] for a in at]
        put(keep_ref, PER_CORE, slot, jnp.where(core == 0, both[0], both[1]))
        put(send_ref, PER_CORE, slot, jnp.where(core == 0, both[1], both[0]))
    for out_ref in (keep_ref, send_ref):
        put(out_ref, PER_CORE, SLOTS - 1, squares[1])


def project(received, norm_gain, new_qkv, other_qkv, old_qkv):
    out = jax.ShapeDtypeStruct((DESTS * SUMS, LANES), f32)
    return pl.pallas_call(
        project_kernel,
        in_specs=[VMEM, VMEM, VMEM, VMEM, ANY],
        out_specs=[VMEM, VMEM],
        out_shape=[out, out],
        scratch_shapes=[
            pltpu.VMEM((FEAT, 2 * USED * HEAD_DIM), bf16),
            pltpu.SemaphoreType.DMA((3,)),
        ],
        compiler_params=params(56),
        name="project",
    )(received, norm_gain.reshape(1, FEAT), new_qkv, other_qkv, old_qkv)


def add_kernel(a_ref, b_ref, out_ref):
    out_ref[...] = a_ref[...] + b_ref[...]


def add(a, b):
    return pl.pallas_call(
        add_kernel,
        in_specs=[VMEM, VMEM],
        out_specs=VMEM,
        out_shape=jax.ShapeDtypeStruct(a.shape, a.dtype),
        compiler_params=params(16),
        name="add",
    )(a, b)


def finish_kernel(x_ref, cos_ref, sin_ref, out_ref):
    parts = x_ref[...].reshape(N_X, HALF_TP, SUMS, LANES)
    late = jnp.sum(jnp.sum(parts[:, :, :HALF_ROWS], axis=1), axis=0)
    early = jnp.sum(parts[:, :, HALF_ROWS:], axis=1)
    summed = jnp.concatenate([early.reshape(HALF_ROWS, LANES), late], axis=0).reshape(
        2, PER_CORE, SLOTS, LANES
    )
    squares = summed[:, :, SLOTS - 1 :, :]
    normed = summed / jnp.sqrt(squares / D + NORM_EPSILON)
    swapped = pltpu.roll(normed.reshape(BLOCK, LANES), HEAD_DIM // 2, 1).reshape(normed.shape)
    rotated = normed * cos_ref[...].reshape(2, 1, 1, LANES) + swapped * sin_ref[...].reshape(
        2, 1, 1, LANES
    )
    slot = lax.broadcasted_iota(jnp.int32, normed.shape, 2)
    result = jnp.where(slot <= GROUP, rotated, jnp.where(slot == GROUP + 1, normed, 0.0))
    out_ref[...] = jnp.broadcast_to(
        result.reshape(1, BLOCK, LANES).astype(bf16), out_ref.shape
    )


def finish(received, cosine, sine):
    return pl.pallas_call(
        finish_kernel,
        in_specs=[VMEM, VMEM, VMEM],
        out_specs=VMEM,
        out_shape=jax.ShapeDtypeStruct((N_TP, BLOCK, LANES), bf16),
        compiler_params=params(16),
        name="finish",
    )(received, cosine, sine)


def attend_kernel(len_ref, q_ref, k_ref, v_ref, out_ref, scores_ref, weights_ref):
    row = pl.program_id(0)
    tp = lax.axis_index("tp")
    chunk = k_ref.shape[1]
    count = STEPS * SLOTS
    blocks = [(row * 2 + s % 2) * 2 for s in range(STEPS)]
    rows_of = [slice(s // 2 * HALF_ROWS, (s // 2 + 1) * HALF_ROWS) for s in range(STEPS)]
    contract_last = (((1,), (1,)), ((), ()))
    by_core = [
        jnp.stack(
            [
                q_ref[b + core, r].astype(f32).reshape(PER_CORE, SLOTS, LANES)
                for b, r in zip(blocks, rows_of)
            ],
            axis=1,
        )
        for core in range(2)
    ]
    wide = jnp.stack(by_core, axis=1).reshape(KV_HEADS, count, LANES)
    queries = [wide[h].astype(bf16) for h in range(KV_HEADS)]
    shifted = [pltpu.roll(wide[h], count - 1, 0).astype(bf16) for h in range(KV_HEADS)]
    new = []
    for h in range(KV_HEADS):
        columns = slice(h * HEAD_DIM, (h + 1) * HEAD_DIM)
        scores_ref[h * count : (h + 1) * count, :] = lax.dot_general(
            queries[h], k_ref[0, :, columns], contract_last, preferred_element_type=f32
        )
        new.append(
            lax.dot_general(queries[h], queries[h], contract_last, preferred_element_type=f32)
        )
    valid = len_ref[row] - tp * chunk
    shape = scores_ref.shape
    position = lax.broadcasted_iota(jnp.int32, shape, 1)
    scores = jnp.where(position < valid, scores_ref[...] * SCORE_SCALE, MASK_VALUE)
    from_step = (lax.broadcasted_iota(jnp.int32, (shape[0], count), 0) >> 3) & (STEPS - 1)
    column = lax.broadcasted_iota(jnp.int32, (shape[0], count), 1)
    new_mask = ((column & (SLOTS - 1)) == GROUP) & ((column >> 3) <= from_step) & (tp == 0)
    scores_new = jnp.where(new_mask, jnp.concatenate(new, axis=0) * SCORE_SCALE, MASK_VALUE)
    peak = jnp.maximum(
        jnp.max(scores, axis=1, keepdims=True), jnp.max(scores_new, axis=1, keepdims=True)
    )
    weights = jnp.exp(scores - peak).astype(bf16)
    weights_new = jnp.exp(scores_new - peak).astype(bf16)
    weights_ref[...] = weights
    total = jnp.sum(weights.astype(f32), axis=1, keepdims=True) + jnp.sum(
        weights_new.astype(f32), axis=1, keepdims=True
    )
    numerator = []
    for h in range(KV_HEADS):
        columns = slice(h * HEAD_DIM, (h + 1) * HEAD_DIM)
        rows = slice(h * count, (h + 1) * count)
        numerator.append(
            jnp.dot(weights_ref[rows, :], v_ref[0, :, columns], preferred_element_type=f32)
            + jnp.dot(weights_new[rows], shifted[h], preferred_element_type=f32)
        )
    grouped = (KV_HEADS, STEPS, SLOTS, LANES)
    part = (jnp.concatenate(numerator, axis=0) / total).reshape(grouped)
    slot = lax.broadcasted_iota(jnp.int32, grouped, 2)
    diagonal = slot == lax.broadcasted_iota(jnp.int32, grouped, 3)
    log_total = jnp.broadcast_to(peak + jnp.log(total), (shape[0], LANES)).reshape(grouped)
    log_row = jnp.sum(jnp.where(diagonal, log_total, 0.0), axis=2, keepdims=True)
    high = log_row.astype(bf16).astype(f32)
    middle = (log_row - high).astype(bf16).astype(f32)
    low = log_row - high - middle
    part = jnp.where(
        slot < GROUP,
        part,
        jnp.where(slot == GROUP, high, jnp.where(slot == GROUP + 1, middle, low)),
    )
    by_core = part.reshape(PER_CORE, 2, STEPS, SLOTS, LANES)
    for core in range(2):
        for s, (b, r) in enumerate(zip(blocks, rows_of)):
            out_ref[b + core, r] = by_core[:, core, s].reshape(HALF_ROWS, LANES).astype(bf16)


def attend(cache_len, gathered, kv_cache):
    chunk = kv_cache.shape[1]
    width = KV_HEADS * HEAD_DIM
    whole = pl.BlockSpec((N_TP, BLOCK, LANES), lambda r: (0, 0, 0))
    lines = KV_HEADS * STEPS * SLOTS
    return pl.pallas_call(
        attend_kernel,
        grid=(ROWS,),
        in_specs=[
            SMEM,
            whole,
            pl.BlockSpec((1, chunk, width), lambda r: (r, 0, 0)),
            pl.BlockSpec((1, chunk, width), lambda r: (r, 0, 1)),
        ],
        out_specs=whole,
        out_shape=jax.ShapeDtypeStruct((N_TP, BLOCK, LANES), bf16),
        scratch_shapes=[pltpu.VMEM((lines, chunk), f32), pltpu.VMEM((lines, chunk), bf16)],
        compiler_params=params(60, 1),
        name="attend",
    )(cache_len, gathered, kv_cache, kv_cache)


def merge_kernel(x_ref, out_ref):
    x = x_ref[...].astype(f32).reshape(N_TP, KV_HEADS, SLOTS, LANES)
    log_row = jnp.sum(x[:, :, GROUP:, :], axis=2, keepdims=True)
    slot = lax.broadcasted_iota(jnp.int32, x.shape, 2)
    lane = lax.broadcasted_iota(jnp.int32, x.shape, 3)
    log_total = jnp.sum(jnp.where(slot == lane, log_row, 0.0), axis=3, keepdims=True)
    share = jnp.exp(log_total - jnp.max(log_total, axis=0, keepdims=True))
    heads = jnp.sum(share * x, axis=0) / jnp.sum(share, axis=0)
    packed = jnp.concatenate([heads[h, :GROUP] for h in range(KV_HEADS)], axis=0)
    out_ref[...] = jnp.broadcast_to(packed.astype(bf16)[None], out_ref.shape)


def merge(received):
    return pl.pallas_call(
        merge_kernel,
        in_specs=[VMEM],
        out_specs=VMEM,
        out_shape=jax.ShapeDtypeStruct((N_TP, HEADS, LANES), bf16),
        compiler_params=params(16),
        name="merge",
    )(received)


def output_kernel(x_ref, old_ref, new_ref, out_ref, wide, heads, early_sum, late_sum):
    step = pl.program_id(0)

    @pl.when(step == 0)
    def _():
        wide[...] = x_ref[...].astype(f32).reshape(wide.shape)
        early_sum[...] = jnp.zeros_like(early_sum)
        late_sum[...] = jnp.zeros_like(late_sum)
        per_step = HEADS // heads.shape[0]
        for h in range(HEADS):
            kv = h // GROUP
            at = kv % 2 * HEADS + kv // 2 * GROUP + h % GROUP
            rows = [wide[pl.ds(at + el * HEADS // 2, HALF_TP, stride=2 * HEADS), :] for el in range(2)]
            at = h % per_step * HEAD_DIM
            heads[h // per_step, :, at : at + HEAD_DIM] = jnp.concatenate(rows, axis=0).astype(
                bf16
            )

    contract_last = (((1,), (1,)), ((), ()))
    both = heads[step]
    early_sum[...] += lax.dot_general(
        both[:HALF_TP], old_ref[...], contract_last, preferred_element_type=f32
    )
    late_sum[...] += lax.dot_general(
        both[HALF_TP:], new_ref[...], contract_last, preferred_element_type=f32
    )

    @pl.when(step == pl.num_programs(0) - 1)
    def _():
        for r in range(ROWS):
            for el, total in enumerate((early_sum, late_sum)):
                out_ref[r, el * 2 : el * 2 + 2, :] = total[r * 2 : r * 2 + 2, :].astype(bf16)


def output(gathered, old_out, fresh_out):
    blocks = 4
    depth = D // blocks
    return pl.pallas_call(
        output_kernel,
        grid=(blocks,),
        in_specs=[
            pl.BlockSpec((N_TP, HEADS, LANES), lambda i: (0, 0, 0)),
            pl.BlockSpec((FEAT, depth), lambda i: (0, i)),
            pl.BlockSpec((FEAT, depth), lambda i: (0, i)),
        ],
        out_specs=pl.BlockSpec((ROWS, STEPS, FEAT), lambda i: (0, 0, 0)),
        out_shape=jax.ShapeDtypeStruct((ROWS, STEPS, FEAT), bf16),
        scratch_shapes=[
            pltpu.VMEM((N_TP * HEADS, LANES), f32),
            pltpu.VMEM((blocks, N_TP, depth), bf16),
            pltpu.VMEM((HALF_TP, FEAT), f32),
            pltpu.VMEM((HALF_TP, FEAT), f32),
        ],
        compiler_params=params(60, 1),
        name="output",
    )(gathered, old_out.T, fresh_out)


def rotation(cache_len):
    tp = lax.axis_index("tp")
    half_dim = HEAD_DIM // 2
    inverse_freq = ROPE_BASE ** (-jnp.arange(half_dim, dtype=f32) * 2.0 / HEAD_DIM)
    positions = cache_len[tp >> 2] + ((tp >> 1) & 1) + 2 * jnp.arange(2, dtype=jnp.int32)
    angles = positions.astype(f32)[:, None] * inverse_freq[None, :]
    cosine, sine = jnp.cos(angles), jnp.sin(angles)
    return (
        jnp.concatenate([cosine, cosine], axis=1),
        jnp.concatenate([-sine, sine], axis=1),
    )


def body(
    token_ids, cache_len, embed_table, norm_gain, old_qkv, old_out, new_qkv, new_out, kv_cache
):
    fresh_out = lax.all_gather(new_out.T, "rep", axis=0, tiled=True)
    other_qkv = lax.ppermute(new_qkv, "rep", [(r, r ^ 1) for r in range(N_REP)])
    cosine, sine = rotation(cache_len)
    rows = lax.all_to_all(gather_rows(token_ids, embed_table), "rep", 0, 0)
    keep, send = project(rows, norm_gain, new_qkv, other_qkv, old_qkv)
    arrived = lax.ppermute(send, "tp", [(t, t ^ 1) for t in range(N_TP)])
    summed = add(keep, arrived).reshape(DESTS, SUMS, LANES)
    groups = [
        [(x * 2 + zh) * N_TP + k * 2 + core for x in range(N_X) for k in range(HALF_TP)]
        for zh in range(2)
        for core in range(2)
    ]
    partials = lax.all_to_all(summed, ("rep", "tp"), 0, 0, axis_index_groups=groups)
    projected = lax.all_to_all(finish(partials, cosine, sine), "tp", 0, 0)
    parts = lax.all_to_all(attend(cache_len, projected, kv_cache), "tp", 0, 0)
    heads = lax.all_to_all(merge(parts), "tp", 0, 0)
    return output(heads, old_out, fresh_out)


def solution(mesh):
    in_specs = (
        P(),
        P("rep"),
        P("rep", "tp"),
        P("tp"),
        P("tp", None),
        P(None, "tp"),
        P(("tp", "rep"), None),
        P(None, ("tp", "rep")),
        P("rep", "tp", None),
    )
    out_specs = P("rep", None, "tp")
    return jax.shard_map(body, mesh=mesh, in_specs=in_specs, out_specs=out_specs, check_vma=False)
```

```python
import functools

import jax
import jax.numpy as jnp
from jax import lax
from jax.experimental import pallas as pl
from jax.experimental.pallas import tpu as pltpu
from jax.sharding import PartitionSpec as P

D = 5120
HEADS = 40
KV_HEADS = 8
HEAD_DIM = 128
GROUP = HEADS // KV_HEADS
STEPS = 4
OLD_STEPS = 2
ROWS = 4
N_REP = 8
N_TP = 16
TOKENS = N_REP * ROWS * STEPS

NORM_EPSILON = 1e-06
ROPE_BASE = 1000000.0
MASK_VALUE = -1e30
SCORE_SCALE = 1.0 / HEAD_DIM**0.5

FEAT = D // N_TP
SHARD = FEAT // N_REP
LANES = 128
HALF_TP = N_TP // 2
N_X = 4
PART = FEAT // N_X
SLOTS = 8
USED = GROUP + 2
BLOCK = KV_HEADS * SLOTS
PER_CORE = KV_HEADS // 2
HALF_ROWS = PER_CORE * SLOTS
SUMS = HALF_ROWS + SLOTS
DESTS = N_X * HALF_TP
WIDE = 3 * LANES

f32 = jnp.float32
bf16 = jnp.bfloat16
MIB = 1 << 20

VMEM = pl.BlockSpec(memory_space=pltpu.VMEM)
SMEM = pl.BlockSpec(memory_space=pltpu.SMEM)
ANY = pl.BlockSpec(memory_space=pl.ANY)


def params(mib, grid=False):
    kwargs = dict(dimension_semantics=("arbitrary",) * grid) if grid else {}
    return pltpu.CompilerParams(vmem_limit_bytes=mib * MIB, **kwargs)

def gather_kernel(ids_ref, tail_ref, table_ref, out_ref, buf, cols, found, sems):
    window = table_ref.shape[1]
    tail_start = window // LANES * LANES
    start = lax.axis_index("rep") * window

    def local_id(i):
        step = ((i >> 5) & 1) * 2 + (i & 1)
        row = ((i >> 3) & 3) * 8 + (i >> 6) * 4 + ((i >> 1) & 3)
        return ids_ref[step, row] - start

    def note(i, count):
        local = local_id(i)
        found[count] = i
        return count + ((local >= 0) & (local < window)).astype(jnp.int32)

    count = lax.fori_loop(0, TOKENS, note, jnp.int32(0), unroll=32)

    def copy(j, local):
        base = pl.multiple_of((local >> 7) << 7, LANES)
        return pltpu.make_async_copy(
            table_ref.at[:, pl.ds(base, LANES)], buf.at[j], sems.at[j]
        )

    def begin(j, carry):
        local = local_id(found[j])

        @pl.when(local < tail_start)
        def _():
            copy(j, local).start()

        return carry

    lax.fori_loop(0, count, begin, 0)
    cols[...] = jnp.zeros_like(cols)
    lane = lax.broadcasted_iota(jnp.int32, (FEAT, LANES), 1)

    def place(i, local, block):
        shift = (i - local) & (LANES - 1)
        moved = pltpu.roll(block.astype(f32), shift, 1)
        cols[:FEAT] = jnp.where(lane == i, moved, cols[:FEAT])

    def end(j, carry):
        i = found[j]
        local = local_id(i)

        @pl.when(local < tail_start)
        def _():
            copy(j, local).wait()
            place(i, local, buf[j])

        @pl.when(local >= tail_start)
        def _():
            place(i, local, tail_ref[...])

        return carry

    lax.fori_loop(0, count, end, 0)
    rows = cols[...].T
    for zh in range(2):
        early = rows[zh * 64 : zh * 64 + DESTS]
        late = rows[zh * 64 + DESTS : zh * 64 + 2 * DESTS]
        tiles = [early[:, n * LANES : (n + 1) * LANES] for n in range(WIDE // LANES)]
        for xx in range(N_X):
            part = late[:, xx * PART : (xx + 1) * PART]
            blank = jnp.zeros((DESTS, LANES - PART), f32)
            block = jnp.concatenate(tiles + [jnp.concatenate([part, blank], axis=1)], axis=0)
            out_ref[xx * 2 + zh] = block.astype(bf16)


def gather_rows(token_ids, embed_table):
    table = embed_table.T
    tail = table.shape[1] // LANES
    return pl.pallas_call(
        gather_kernel,
        grid=(1,),
        in_specs=[SMEM, pl.BlockSpec((FEAT, LANES), lambda i: (0, tail)), ANY],
        out_specs=VMEM,
        out_shape=jax.ShapeDtypeStruct((N_REP, 4 * DESTS, LANES), bf16),
        scratch_shapes=[
            pltpu.VMEM((TOKENS, FEAT, LANES), bf16),
            pltpu.VMEM((WIDE, LANES), f32),
            pltpu.SMEM((TOKENS,), jnp.int32),
            pltpu.SemaphoreType.DMA((TOKENS,)),
        ],
        compiler_params=params(55),
        name="gather_rows",
    )(token_ids.T, table, table)


def old_columns_kernel(old_ref, out_ref, sems):
    xx = lax.axis_index("rep") >> 1
    copies = []
    for n, (first, width, to) in enumerate(
        (
            (0, 2 * GROUP, 0),
            (HEADS, 2, 2 * GROUP),
            (HEADS + KV_HEADS, 2, 2 * GROUP + 2),
        )
    ):
        at = pl.multiple_of((first + xx * width) * HEAD_DIM, HEAD_DIM)
        copies.append(
            pltpu.make_async_copy(
                old_ref.at[:, pl.ds(at, width * HEAD_DIM)],
                out_ref.at[:, pl.ds(to * HEAD_DIM, width * HEAD_DIM)],
                sems.at[n],
            )
        )
        copies[-1].start()
    for copy in copies:
        copy.wait()


def take_old_columns(old_qkv):
    shape = (FEAT, 2 * USED * HEAD_DIM)
    return pl.pallas_call(
        old_columns_kernel,
        in_specs=[ANY],
        out_specs=VMEM,
        out_shape=jax.ShapeDtypeStruct(shape, bf16),
        scratch_shapes=[pltpu.SemaphoreType.DMA((3,))],
        compiler_params=params(8),
        cost_estimate=pl.CostEstimate(
            flops=0, bytes_accessed=4 * shape[0] * shape[1], transcendentals=0
        ),
        name="take_old_columns",
    )(old_qkv)


def project_kernel(x_ref, gain_ref, new_ref, other_ref, old, keep_ref, send_ref):
    rep, core = lax.axis_index("rep"), lax.axis_index("tp") & 1
    xx, zh = rep >> 1, rep & 1
    embedded = jnp.sum(x_ref[...].astype(f32), axis=0)
    early = jnp.concatenate(
        [embedded[n * DESTS : (n + 1) * DESTS] for n in range(WIDE // LANES)], axis=1
    )
    late = embedded[3 * DESTS :]
    squares = [
        jnp.broadcast_to(jnp.sum(e * e, axis=1, keepdims=True), (DESTS, LANES))
        for e in (late, early)
    ]
    gain = gain_ref[...].astype(f32)
    part_gain = jnp.zeros((1, PART), f32)
    for i in range(N_X):
        part_gain = part_gain + jnp.where(xx == i, gain[:, i * PART : (i + 1) * PART], 0.0)
    early = (early[:, :FEAT] * gain).astype(bf16)
    late = (late[:, :PART] * part_gain).astype(bf16)
    first, second = late[:, :SHARD], late[:, SHARD:]
    late_own = jnp.where(zh == 0, first, second)
    late_other = jnp.where(zh == 0, second, first)

    def put(out_ref, group, slot, value):
        out_ref[pl.ds(group * SLOTS + slot, DESTS, stride=SUMS), :] = value

    for out_ref, side in ((keep_ref, core), (send_ref, 1 - core)):
        for j in range(PER_CORE):
            head = j * 2 + side
            starts = (
                (head * (GROUP * HEAD_DIM), GROUP, 0),
                (HEADS * HEAD_DIM + head * HEAD_DIM, 1, GROUP),
                ((HEADS + KV_HEADS) * HEAD_DIM + head * HEAD_DIM, 1, GROUP + 1),
            )
            for start, width, slot in starts:
                columns = pl.ds(pl.multiple_of(start, HEAD_DIM), width * HEAD_DIM)
                sums = jnp.dot(
                    late_own, new_ref[:, columns], preferred_element_type=f32
                ) + jnp.dot(late_other, other_ref[:, columns], preferred_element_type=f32)
                for g in range(width):
                    put(out_ref, j, slot + g, sums[:, g * HEAD_DIM : (g + 1) * HEAD_DIM])
            put(out_ref, j, SLOTS - 1, squares[0])
    sums = jnp.dot(early, old[...], preferred_element_type=f32)
    for slot in range(USED):
        at = (slot, slot + GROUP) if slot < GROUP else (slot * 2, slot * 2 + 1)
        both = [sums[:, a * HEAD_DIM : (a + 1) * HEAD_DIM] for a in at]
        put(keep_ref, PER_CORE, slot, jnp.where(core == 0, both[0], both[1]))
        put(send_ref, PER_CORE, slot, jnp.where(core == 0, both[1], both[0]))
    for out_ref in (keep_ref, send_ref):
        put(out_ref, PER_CORE, SLOTS - 1, squares[1])


def project(received, norm_gain, new_qkv, other_qkv, old_columns):
    out = jax.ShapeDtypeStruct((DESTS * SUMS, LANES), f32)
    return pl.pallas_call(
        project_kernel,
        in_specs=[VMEM] * 5,
        out_specs=[VMEM, VMEM],
        out_shape=[out, out],
        compiler_params=params(16),
        name="project",
    )(received, norm_gain.reshape(1, FEAT), new_qkv, other_qkv, old_columns)


def add_kernel(a_ref, b_ref, out_ref):
    out_ref[...] = a_ref[...] + b_ref[...]


def add(a, b):
    return pl.pallas_call(
        add_kernel,
        in_specs=[VMEM, VMEM],
        out_specs=VMEM,
        out_shape=jax.ShapeDtypeStruct(a.shape, a.dtype),
        compiler_params=params(16),
        name="add",
    )(a, b)


def finish_kernel(x_ref, cos_ref, sin_ref, out_ref):
    parts = x_ref[...].reshape(N_X, HALF_TP, SUMS, LANES)
    late = jnp.sum(jnp.sum(parts[:, :, :HALF_ROWS], axis=1), axis=0)
    early = jnp.sum(parts[:, :, HALF_ROWS:], axis=1)
    summed = jnp.concatenate([early.reshape(HALF_ROWS, LANES), late], axis=0).reshape(
        2, PER_CORE, SLOTS, LANES
    )
    squares = summed[:, :, SLOTS - 1 :, :]
    normed = summed / jnp.sqrt(squares / D + NORM_EPSILON)
    swapped = pltpu.roll(normed.reshape(BLOCK, LANES), HEAD_DIM // 2, 1).reshape(normed.shape)
    rotated = normed * cos_ref[...].reshape(2, 1, 1, LANES) + swapped * sin_ref[...].reshape(
        2, 1, 1, LANES
    )
    slot = lax.broadcasted_iota(jnp.int32, normed.shape, 2)
    result = jnp.where(slot <= GROUP, rotated, jnp.where(slot == GROUP + 1, normed, 0.0))
    out_ref[...] = jnp.broadcast_to(
        result.reshape(1, BLOCK, LANES).astype(bf16), out_ref.shape
    )


def finish(received, cosine, sine):
    return pl.pallas_call(
        finish_kernel,
        in_specs=[VMEM, VMEM, VMEM],
        out_specs=VMEM,
        out_shape=jax.ShapeDtypeStruct((N_TP, BLOCK, LANES), bf16),
        compiler_params=params(16),
        cost_estimate=pl.CostEstimate(flops=0, bytes_accessed=32 * MIB, transcendentals=0),
        name="finish",
    )(received, cosine, sine)


def attend_kernel(len_ref, q_ref, kv_ref, out_ref, scores_ref, weights_ref):
    row = pl.program_id(0)
    tp = lax.axis_index("tp")
    chunk = kv_ref.shape[1]
    value_at = KV_HEADS * HEAD_DIM
    count = STEPS * SLOTS
    blocks = [(row * 2 + s % 2) * 2 for s in range(STEPS)]
    rows_of = [slice(s // 2 * HALF_ROWS, (s // 2 + 1) * HALF_ROWS) for s in range(STEPS)]
    contract_last = (((1,), (1,)), ((), ()))
    by_core = [
        jnp.stack(
            [
                q_ref[b + core, r].astype(f32).reshape(PER_CORE, SLOTS, LANES)
                for b, r in zip(blocks, rows_of)
            ],
            axis=1,
        )
        for core in range(2)
    ]
    wide = jnp.stack(by_core, axis=1).reshape(KV_HEADS, count, LANES)
    queries = [wide[h].astype(bf16) for h in range(KV_HEADS)]
    shifted = [pltpu.roll(wide[h], count - 1, 0).astype(bf16) for h in range(KV_HEADS)]
    new = []
    for h in range(KV_HEADS):
        columns = slice(h * HEAD_DIM, (h + 1) * HEAD_DIM)
        scores_ref[h * count : (h + 1) * count, :] = lax.dot_general(
            queries[h], kv_ref[row, :, columns], contract_last, preferred_element_type=f32
        )
        new.append(
            lax.dot_general(queries[h], queries[h], contract_last, preferred_element_type=f32)
        )
    valid = len_ref[row] - tp * chunk
    shape = scores_ref.shape
    position = lax.broadcasted_iota(jnp.int32, shape, 1)
    scores = jnp.where(position < valid, scores_ref[...] * SCORE_SCALE, MASK_VALUE)
    from_step = (lax.broadcasted_iota(jnp.int32, (shape[0], count), 0) >> 3) & (STEPS - 1)
    column = lax.broadcasted_iota(jnp.int32, (shape[0], count), 1)
    new_mask = ((column & (SLOTS - 1)) == GROUP) & ((column >> 3) <= from_step) & (tp == 0)
    scores_new = jnp.where(new_mask, jnp.concatenate(new, axis=0) * SCORE_SCALE, MASK_VALUE)
    peak = jnp.maximum(
        jnp.max(scores, axis=1, keepdims=True), jnp.max(scores_new, axis=1, keepdims=True)
    )
    weights = jnp.exp(scores - peak).astype(bf16)
    weights_new = jnp.exp(scores_new - peak).astype(bf16)
    weights_ref[...] = weights
    total = jnp.sum(weights.astype(f32), axis=1, keepdims=True) + jnp.sum(
        weights_new.astype(f32), axis=1, keepdims=True
    )
    numerator = []
    for h in range(KV_HEADS):
        columns = slice(value_at + h * HEAD_DIM, value_at + (h + 1) * HEAD_DIM)
        rows = slice(h * count, (h + 1) * count)
        numerator.append(
            jnp.dot(weights_ref[rows, :], kv_ref[row, :, columns], preferred_element_type=f32)
            + jnp.dot(weights_new[rows], shifted[h], preferred_element_type=f32)
        )
    grouped = (KV_HEADS, STEPS, SLOTS, LANES)
    part = (jnp.concatenate(numerator, axis=0) / total).reshape(grouped)
    slot = lax.broadcasted_iota(jnp.int32, grouped, 2)
    diagonal = slot == lax.broadcasted_iota(jnp.int32, grouped, 3)
    log_total = jnp.broadcast_to(peak + jnp.log(total), (shape[0], LANES)).reshape(grouped)
    log_row = jnp.sum(jnp.where(diagonal, log_total, 0.0), axis=2, keepdims=True)
    high = log_row.astype(bf16).astype(f32)
    middle = (log_row - high).astype(bf16).astype(f32)
    low = log_row - high - middle
    part = jnp.where(
        slot < GROUP,
        part,
        jnp.where(slot == GROUP, high, jnp.where(slot == GROUP + 1, middle, low)),
    )
    by_core = part.reshape(PER_CORE, 2, STEPS, SLOTS, LANES)
    for core in range(2):
        for s, (b, r) in enumerate(zip(blocks, rows_of)):
            out_ref[b + core, r] = by_core[:, core, s].reshape(HALF_ROWS, LANES).astype(bf16)


def attend(cache_len, gathered, kv_cache):
    chunk = kv_cache.shape[1]
    whole = pl.BlockSpec((N_TP, BLOCK, LANES), lambda r: (0, 0, 0))
    lines = KV_HEADS * STEPS * SLOTS
    return pl.pallas_call(
        attend_kernel,
        grid=(ROWS,),
        in_specs=[
            SMEM,
            whole,
            VMEM,
        ],
        out_specs=whole,
        out_shape=jax.ShapeDtypeStruct((N_TP, BLOCK, LANES), bf16),
        scratch_shapes=[pltpu.VMEM((lines, chunk), f32), pltpu.VMEM((lines, chunk), bf16)],
        compiler_params=params(16, 1),
        name="attend",
    )(cache_len, gathered, kv_cache)


def merge_kernel(x_ref, out_ref):
    x = x_ref[...].astype(f32).reshape(N_TP, KV_HEADS, SLOTS, LANES)
    log_row = jnp.sum(x[:, :, GROUP:, :], axis=2, keepdims=True)
    slot = lax.broadcasted_iota(jnp.int32, x.shape, 2)
    lane = lax.broadcasted_iota(jnp.int32, x.shape, 3)
    log_total = jnp.sum(jnp.where(slot == lane, log_row, 0.0), axis=3, keepdims=True)
    share = jnp.exp(log_total - jnp.max(log_total, axis=0, keepdims=True))
    heads = jnp.sum(share * x, axis=0) / jnp.sum(share, axis=0)
    packed = jnp.concatenate([heads[h, :GROUP] for h in range(KV_HEADS)], axis=0)
    out_ref[...] = jnp.broadcast_to(packed.astype(bf16)[None], out_ref.shape)


def merge(received):
    return pl.pallas_call(
        merge_kernel,
        in_specs=[VMEM],
        out_specs=VMEM,
        out_shape=jax.ShapeDtypeStruct((N_TP, HEADS, LANES), bf16),
        compiler_params=params(16),
        name="merge",
    )(received)


def output_kernel(*refs):
    x_ref, old_ref, *pieces, out_ref, wide, heads, late_parts = refs
    rep = lax.axis_index("rep")
    xx, zh = rep >> 1, rep & 1
    wide[...] = x_ref[...].astype(f32).reshape(wide.shape)
    for h in range(HEADS):
        kv = h // GROUP
        at = kv % 2 * HEADS + kv // 2 * GROUP + h % GROUP
        rows = [
            wide[pl.ds(at + el * HEADS // 2, HALF_TP, stride=2 * HEADS), :] for el in range(2)
        ]
        heads[:, h * HEAD_DIM : (h + 1) * HEAD_DIM] = jnp.concatenate(rows, axis=0).astype(bf16)
    contract_last = (((1,), (1,)), ((), ()))
    early_heads, late_heads = heads[:HALF_TP], heads[HALF_TP:]
    for n, piece in enumerate(pieces):
        place = ((xx + n // 2) & (N_X - 1)) * 2 + (zh ^ (n & 1))
        late_parts[place, :, :SHARD] = lax.dot_general(
            late_heads, piece[...], contract_last, preferred_element_type=f32
        )
    early = lax.dot_general(
        early_heads, old_ref[...], contract_last, preferred_element_type=f32
    )
    late = jnp.concatenate([late_parts[r, :, :SHARD] for r in range(N_REP)], axis=1)
    for r in range(ROWS):
        for el, total in enumerate((early, late)):
            out_ref[r, el * 2 : el * 2 + 2, :] = total[r * 2 : r * 2 + 2, :].astype(bf16)


def output(gathered, old_out, pieces):
    return pl.pallas_call(
        output_kernel,
        in_specs=[VMEM] * (2 + N_REP),
        out_specs=VMEM,
        out_shape=jax.ShapeDtypeStruct((ROWS, STEPS, FEAT), bf16),
        scratch_shapes=[
            pltpu.VMEM((N_TP * HEADS, LANES), f32),
            pltpu.VMEM((N_TP, D), bf16),
            pltpu.VMEM((N_REP, HALF_TP, LANES), f32),
        ],
        compiler_params=params(16),
        name="output",
    )(gathered, old_out.T, *pieces)


def rotation(cache_len):
    tp = lax.axis_index("tp")
    half_dim = HEAD_DIM // 2
    inverse_freq = ROPE_BASE ** (-jnp.arange(half_dim, dtype=f32) * 2.0 / HEAD_DIM)
    positions = cache_len[tp >> 2] + ((tp >> 1) & 1) + 2 * jnp.arange(2, dtype=jnp.int32)
    angles = positions.astype(f32)[:, None] * inverse_freq[None, :]
    cosine, sine = jnp.cos(angles), jnp.sin(angles)
    return (
        jnp.concatenate([cosine, cosine], axis=1),
        jnp.concatenate([-sine, sine], axis=1),
    )


def body(
    token_ids, cache_len, embed_table, norm_gain, old_qkv, old_out, new_qkv, new_out, kv_cache
):
    turn = [(r, r ^ 1) for r in range(N_REP)]
    ahead = [(r, (r + 2) % N_REP) for r in range(N_REP)]
    back = [(r, (r - 2) % N_REP) for r in range(N_REP)]
    other_qkv = lax.ppermute(new_qkv, "rep", turn)
    cosine, sine = rotation(cache_len)
    rows = gather_rows(token_ids, embed_table)
    rows, old_qkv = lax.optimization_barrier((rows, old_qkv))
    old_columns = take_old_columns(old_qkv)
    rows = lax.all_to_all(rows, "rep", 0, 0)
    rows, old_columns, cosine, sine = lax.optimization_barrier((rows, old_columns, cosine, sine))
    keep, send = project(rows, norm_gain, new_qkv, other_qkv, old_columns)
    arrived = lax.ppermute(send, "tp", [(t, t ^ 1) for t in range(N_TP)])
    summed = add(keep, arrived).reshape(DESTS, SUMS, LANES)
    groups = [
        [(x * 2 + zh) * N_TP + k * 2 + core for x in range(N_X) for k in range(HALF_TP)]
        for zh in range(2)
        for core in range(2)
    ]
    partials = lax.all_to_all(summed, ("rep", "tp"), 0, 0, axis_index_groups=groups)
    partials, own = lax.optimization_barrier((partials, new_out.T))
    other = lax.ppermute(own, "rep", turn)
    behind_own = lax.ppermute(own, "rep", ahead)
    front_own = lax.ppermute(own, "rep", back)
    projected = lax.all_to_all(finish(partials, cosine, sine), "tp", 0, 0)
    projected, other, behind_own = lax.optimization_barrier((projected, other, behind_own))
    far_own = lax.ppermute(behind_own, "rep", ahead)
    front_other = lax.ppermute(other, "rep", back)
    parts = lax.all_to_all(attend(cache_len, projected, kv_cache), "tp", 0, 0)
    parts, front_other, other = lax.optimization_barrier((parts, front_other, other))
    far_other = lax.ppermute(front_other, "rep", back)
    behind_other = lax.ppermute(other, "rep", ahead)
    heads = lax.all_to_all(merge(parts), "tp", 0, 0)
    pieces = (
        own,
        other,
        front_own,
        front_other,
        far_own,
        far_other,
        behind_own,
        behind_other,
    )
    return output(heads, old_out, pieces)


def solution(mesh):
    in_specs = (
        P(),
        P("rep"),
        P("rep", "tp"),
        P("tp"),
        P("tp", None),
        P(None, "tp"),
        P(("tp", "rep"), None),
        P(None, ("tp", "rep")),
        P("rep", "tp", None),
    )
    out_specs = P("rep", None, "tp")
    return jax.shard_map(body, mesh=mesh, in_specs=in_specs, out_specs=out_specs, check_vma=False)
```

```python
import functools

import jax
import jax.numpy as jnp
from jax import lax
from jax.experimental import pallas as pl
from jax.experimental.pallas import tpu as pltpu
from jax.sharding import PartitionSpec as P

D = 5120
HEADS = 40
KV_HEADS = 8
HEAD_DIM = 128
GROUP = HEADS // KV_HEADS
STEPS = 4
OLD_STEPS = 2
ROWS = 4
N_REP = 8
N_TP = 16
TOKENS = N_REP * ROWS * STEPS

NORM_EPSILON = 1e-06
ROPE_BASE = 1000000.0
MASK_VALUE = -1e30
SCORE_SCALE = 1.0 / HEAD_DIM**0.5

FEAT = D // N_TP
SHARD = FEAT // N_REP
LANES = 128
HALF_TP = N_TP // 2
N_X = 4
PART = FEAT // N_X
SLOTS = 8
USED = GROUP + 2
BLOCK = KV_HEADS * SLOTS
PER_CORE = KV_HEADS // 2
HALF_ROWS = PER_CORE * SLOTS
SUMS = HALF_ROWS + SLOTS
DESTS = N_X * HALF_TP
WIDE = 3 * LANES

f32 = jnp.float32
bf16 = jnp.bfloat16
MIB = 1 << 20

VMEM = pl.BlockSpec(memory_space=pltpu.VMEM)
SMEM = pl.BlockSpec(memory_space=pltpu.SMEM)
ANY = pl.BlockSpec(memory_space=pl.ANY)


def params(mib, grid=False):
    kwargs = dict(dimension_semantics=("arbitrary",) * grid) if grid else {}
    return pltpu.CompilerParams(vmem_limit_bytes=int(mib * MIB), **kwargs)

def gather_kernel(ids_ref, tail_ref, table_ref, out_ref, buf, cols, found, sems):
    window = table_ref.shape[1]
    tail_start = window // LANES * LANES
    start = lax.axis_index("rep") * window

    def local_id(i):
        step = ((i >> 5) & 1) * 2 + (i & 1)
        row = ((i >> 3) & 3) * 8 + (i >> 6) * 4 + ((i >> 1) & 3)
        return ids_ref[step, row] - start

    def note(i, count):
        local = local_id(i)
        found[count] = i
        return count + ((local >= 0) & (local < window)).astype(jnp.int32)

    count = lax.fori_loop(0, TOKENS, note, jnp.int32(0), unroll=32)

    def copy(j, local):
        base = pl.multiple_of((local >> 7) << 7, LANES)
        return pltpu.make_async_copy(
            table_ref.at[:, pl.ds(base, LANES)], buf.at[j], sems.at[j]
        )

    def begin(j, carry):
        local = local_id(found[j])

        @pl.when(local < tail_start)
        def _():
            copy(j, local).start()

        return carry

    lax.fori_loop(0, count, begin, 0)
    cols[...] = jnp.zeros_like(cols)
    lane = lax.broadcasted_iota(jnp.int32, (FEAT, LANES), 1)

    def place(i, local, block):
        shift = (i - local) & (LANES - 1)
        moved = pltpu.roll(block.astype(f32), shift, 1)
        cols[:FEAT] = jnp.where(lane == i, moved, cols[:FEAT])

    def end(j, carry):
        i = found[j]
        local = local_id(i)

        @pl.when(local < tail_start)
        def _():
            copy(j, local).wait()
            place(i, local, buf[j])

        @pl.when(local >= tail_start)
        def _():
            place(i, local, tail_ref[...])

        return carry

    lax.fori_loop(0, count, end, 0)
    rows = cols[...].T
    for zh in range(2):
        early = rows[zh * 64 : zh * 64 + DESTS]
        late = rows[zh * 64 + DESTS : zh * 64 + 2 * DESTS]
        tiles = [early[:, n * LANES : (n + 1) * LANES] for n in range(WIDE // LANES)]
        for xx in range(N_X):
            part = late[:, xx * PART : (xx + 1) * PART]
            blank = jnp.zeros((DESTS, LANES - PART), f32)
            block = jnp.concatenate(tiles + [jnp.concatenate([part, blank], axis=1)], axis=0)
            out_ref[xx * 2 + zh] = block.astype(bf16)


def gather_rows(token_ids, embed_table):
    table = embed_table.T
    tail = table.shape[1] // LANES
    return pl.pallas_call(
        gather_kernel,
        grid=(1,),
        in_specs=[SMEM, pl.BlockSpec((FEAT, LANES), lambda i: (0, tail)), ANY],
        out_specs=VMEM,
        out_shape=jax.ShapeDtypeStruct((N_REP, 4 * DESTS, LANES), bf16),
        scratch_shapes=[
            pltpu.VMEM((TOKENS, FEAT, LANES), bf16),
            pltpu.VMEM((WIDE, LANES), f32),
            pltpu.SMEM((TOKENS,), jnp.int32),
            pltpu.SemaphoreType.DMA((TOKENS,)),
        ],
        compiler_params=params(55),
        name="gather_rows",
    )(token_ids.T, table, table)


def old_columns_kernel(old_ref, out_ref, sems):
    xx = lax.axis_index("rep") >> 1
    copies = []
    for n, (first, width, to) in enumerate(
        (
            (0, 2 * GROUP, 0),
            (HEADS, 2, 2 * GROUP),
            (HEADS + KV_HEADS, 2, 2 * GROUP + 2),
        )
    ):
        at = pl.multiple_of((first + xx * width) * HEAD_DIM, HEAD_DIM)
        copies.append(
            pltpu.make_async_copy(
                old_ref.at[:, pl.ds(at, width * HEAD_DIM)],
                out_ref.at[:, pl.ds(to * HEAD_DIM, width * HEAD_DIM)],
                sems.at[n],
            )
        )
        copies[-1].start()
    for copy in copies:
        copy.wait()


def take_old_columns(old_qkv):
    shape = (FEAT, 2 * USED * HEAD_DIM)
    return pl.pallas_call(
        old_columns_kernel,
        in_specs=[ANY],
        out_specs=VMEM,
        out_shape=jax.ShapeDtypeStruct(shape, bf16),
        scratch_shapes=[pltpu.SemaphoreType.DMA((3,))],
        compiler_params=params(8),
        cost_estimate=pl.CostEstimate(
            flops=0, bytes_accessed=4 * shape[0] * shape[1], transcendentals=0
        ),
        name="take_old_columns",
    )(old_qkv)


def project_kernel(x_ref, gain_ref, new_ref, other_ref, old, keep_ref, send_ref):
    rep, core = lax.axis_index("rep"), lax.axis_index("tp") & 1
    xx, zh = rep >> 1, rep & 1
    embedded = jnp.sum(x_ref[...].astype(f32), axis=0)
    early = jnp.concatenate(
        [embedded[n * DESTS : (n + 1) * DESTS] for n in range(WIDE // LANES)], axis=1
    )
    late = embedded[3 * DESTS :]
    squares = [
        jnp.broadcast_to(jnp.sum(e * e, axis=1, keepdims=True), (DESTS, LANES))
        for e in (late, early)
    ]
    gain = gain_ref[...].astype(f32)
    part_gain = jnp.zeros((1, PART), f32)
    for i in range(N_X):
        part_gain = part_gain + jnp.where(xx == i, gain[:, i * PART : (i + 1) * PART], 0.0)
    early = (early[:, :FEAT] * gain).astype(bf16)
    late = (late[:, :PART] * part_gain).astype(bf16)
    first, second = late[:, :SHARD], late[:, SHARD:]
    late_own = jnp.where(zh == 0, first, second)
    late_other = jnp.where(zh == 0, second, first)

    def put(out_ref, group, slot, value):
        out_ref[pl.ds(group * SLOTS + slot, DESTS, stride=SUMS), :] = value

    for out_ref, side in ((keep_ref, core), (send_ref, 1 - core)):
        for j in range(PER_CORE):
            head = j * 2 + side
            starts = (
                (head * (GROUP * HEAD_DIM), GROUP, 0),
                (HEADS * HEAD_DIM + head * HEAD_DIM, 1, GROUP),
                ((HEADS + KV_HEADS) * HEAD_DIM + head * HEAD_DIM, 1, GROUP + 1),
            )
            for start, width, slot in starts:
                columns = pl.ds(pl.multiple_of(start, HEAD_DIM), width * HEAD_DIM)
                sums = jnp.dot(
                    late_own, new_ref[:, columns], preferred_element_type=f32
                ) + jnp.dot(late_other, other_ref[:, columns], preferred_element_type=f32)
                for g in range(width):
                    put(out_ref, j, slot + g, sums[:, g * HEAD_DIM : (g + 1) * HEAD_DIM])
            put(out_ref, j, SLOTS - 1, squares[0])
    sums = jnp.dot(early, old[...], preferred_element_type=f32)
    for slot in range(USED):
        at = (slot, slot + GROUP) if slot < GROUP else (slot * 2, slot * 2 + 1)
        both = [sums[:, a * HEAD_DIM : (a + 1) * HEAD_DIM] for a in at]
        put(keep_ref, PER_CORE, slot, jnp.where(core == 0, both[0], both[1]))
        put(send_ref, PER_CORE, slot, jnp.where(core == 0, both[1], both[0]))
    for out_ref in (keep_ref, send_ref):
        put(out_ref, PER_CORE, SLOTS - 1, squares[1])


def project(received, norm_gain, new_qkv, other_qkv, old_columns):
    out = jax.ShapeDtypeStruct((DESTS * SUMS, LANES), f32)
    return pl.pallas_call(
        project_kernel,
        in_specs=[VMEM] * 5,
        out_specs=[VMEM, VMEM],
        out_shape=[out, out],
        compiler_params=params(16),
        name="project",
    )(received, norm_gain.reshape(1, FEAT), new_qkv, other_qkv, old_columns)


def add_kernel(a_ref, b_ref, out_ref):
    out_ref[...] = a_ref[...] + b_ref[...]


def add(a, b):
    return pl.pallas_call(
        add_kernel,
        in_specs=[VMEM, VMEM],
        out_specs=VMEM,
        out_shape=jax.ShapeDtypeStruct(a.shape, a.dtype),
        compiler_params=params(16),
        name="add",
    )(a, b)


def finish_kernel(x_ref, cos_ref, sin_ref, *refs):
    out_ref = refs[-1]
    parts = x_ref[...].reshape(N_X, HALF_TP, SUMS, LANES)
    late = jnp.sum(jnp.sum(parts[:, :, :HALF_ROWS], axis=1), axis=0)
    early = jnp.sum(parts[:, :, HALF_ROWS:], axis=1)
    summed = jnp.concatenate([early.reshape(HALF_ROWS, LANES), late], axis=0).reshape(
        2, PER_CORE, SLOTS, LANES
    )
    squares = summed[:, :, SLOTS - 1 :, :]
    normed = summed / jnp.sqrt(squares / D + NORM_EPSILON)
    swapped = pltpu.roll(normed.reshape(BLOCK, LANES), HEAD_DIM // 2, 1).reshape(normed.shape)
    rotated = normed * cos_ref[...].reshape(2, 1, 1, LANES) + swapped * sin_ref[...].reshape(
        2, 1, 1, LANES
    )
    slot = lax.broadcasted_iota(jnp.int32, normed.shape, 2)
    result = jnp.where(slot <= GROUP, rotated, jnp.where(slot == GROUP + 1, normed, 0.0))
    out_ref[...] = jnp.broadcast_to(
        result.reshape(1, BLOCK, LANES).astype(bf16), out_ref.shape
    )


def finish(received, cosine, sine, *far):
    return pl.pallas_call(
        finish_kernel,
        in_specs=[VMEM, VMEM, VMEM] + [ANY] * len(far),
        out_specs=VMEM,
        out_shape=jax.ShapeDtypeStruct((N_TP, BLOCK, LANES), bf16),
        compiler_params=params(53.5),
        name="finish",
    )(received, cosine, sine, *far)


def attend_kernel(len_ref, q_ref, kv_ref, out_ref, scores_ref, weights_ref):
    row = pl.program_id(0)
    tp = lax.axis_index("tp")
    chunk = kv_ref.shape[1]
    value_at = KV_HEADS * HEAD_DIM
    count = STEPS * SLOTS
    blocks = [(row * 2 + s % 2) * 2 for s in range(STEPS)]
    rows_of = [slice(s // 2 * HALF_ROWS, (s // 2 + 1) * HALF_ROWS) for s in range(STEPS)]
    contract_last = (((1,), (1,)), ((), ()))
    by_core = [
        jnp.stack(
            [
                q_ref[b + core, r].astype(f32).reshape(PER_CORE, SLOTS, LANES)
                for b, r in zip(blocks, rows_of)
            ],
            axis=1,
        )
        for core in range(2)
    ]
    wide = jnp.stack(by_core, axis=1).reshape(KV_HEADS, count, LANES)
    queries = [wide[h].astype(bf16) for h in range(KV_HEADS)]
    shifted = [pltpu.roll(wide[h], count - 1, 0).astype(bf16) for h in range(KV_HEADS)]
    new = []
    for h in range(KV_HEADS):
        columns = slice(h * HEAD_DIM, (h + 1) * HEAD_DIM)
        scores_ref[h * count : (h + 1) * count, :] = lax.dot_general(
            queries[h], kv_ref[row, :, columns], contract_last, preferred_element_type=f32
        )
        new.append(
            lax.dot_general(queries[h], queries[h], contract_last, preferred_element_type=f32)
        )
    valid = len_ref[row] - tp * chunk
    shape = scores_ref.shape
    position = lax.broadcasted_iota(jnp.int32, shape, 1)
    scores = jnp.where(position < valid, scores_ref[...] * SCORE_SCALE, MASK_VALUE)
    from_step = (lax.broadcasted_iota(jnp.int32, (shape[0], count), 0) >> 3) & (STEPS - 1)
    column = lax.broadcasted_iota(jnp.int32, (shape[0], count), 1)
    new_mask = ((column & (SLOTS - 1)) == GROUP) & ((column >> 3) <= from_step) & (tp == 0)
    scores_new = jnp.where(new_mask, jnp.concatenate(new, axis=0) * SCORE_SCALE, MASK_VALUE)
    peak = jnp.maximum(
        jnp.max(scores, axis=1, keepdims=True), jnp.max(scores_new, axis=1, keepdims=True)
    )
    weights = jnp.exp(scores - peak).astype(bf16)
    weights_new = jnp.exp(scores_new - peak).astype(bf16)
    weights_ref[...] = weights
    total = jnp.sum(weights.astype(f32), axis=1, keepdims=True) + jnp.sum(
        weights_new.astype(f32), axis=1, keepdims=True
    )
    numerator = []
    for h in range(KV_HEADS):
        columns = slice(value_at + h * HEAD_DIM, value_at + (h + 1) * HEAD_DIM)
        rows = slice(h * count, (h + 1) * count)
        numerator.append(
            jnp.dot(weights_ref[rows, :], kv_ref[row, :, columns], preferred_element_type=f32)
            + jnp.dot(weights_new[rows], shifted[h], preferred_element_type=f32)
        )
    grouped = (KV_HEADS, STEPS, SLOTS, LANES)
    part = (jnp.concatenate(numerator, axis=0) / total).reshape(grouped)
    slot = lax.broadcasted_iota(jnp.int32, grouped, 2)
    diagonal = slot == lax.broadcasted_iota(jnp.int32, grouped, 3)
    log_total = jnp.broadcast_to(peak + jnp.log(total), (shape[0], LANES)).reshape(grouped)
    log_row = jnp.sum(jnp.where(diagonal, log_total, 0.0), axis=2, keepdims=True)
    high = log_row.astype(bf16).astype(f32)
    middle = (log_row - high).astype(bf16).astype(f32)
    low = log_row - high - middle
    part = jnp.where(
        slot < GROUP,
        part,
        jnp.where(slot == GROUP, high, jnp.where(slot == GROUP + 1, middle, low)),
    )
    by_core = part.reshape(PER_CORE, 2, STEPS, SLOTS, LANES)
    for core in range(2):
        for s, (b, r) in enumerate(zip(blocks, rows_of)):
            out_ref[b + core, r] = by_core[:, core, s].reshape(HALF_ROWS, LANES).astype(bf16)


def attend(cache_len, gathered, kv_cache):
    chunk = kv_cache.shape[1]
    whole = pl.BlockSpec((N_TP, BLOCK, LANES), lambda r: (0, 0, 0))
    lines = KV_HEADS * STEPS * SLOTS
    return pl.pallas_call(
        attend_kernel,
        grid=(ROWS,),
        in_specs=[
            SMEM,
            whole,
            VMEM,
        ],
        out_specs=whole,
        out_shape=jax.ShapeDtypeStruct((N_TP, BLOCK, LANES), bf16),
        scratch_shapes=[pltpu.VMEM((lines, chunk), f32), pltpu.VMEM((lines, chunk), bf16)],
        compiler_params=params(16, 1),
        name="attend",
    )(cache_len, gathered, kv_cache)


def merge_kernel(x_ref, out_ref):
    x = x_ref[...].astype(f32).reshape(N_TP, KV_HEADS, SLOTS, LANES)
    log_row = jnp.sum(x[:, :, GROUP:, :], axis=2, keepdims=True)
    slot = lax.broadcasted_iota(jnp.int32, x.shape, 2)
    lane = lax.broadcasted_iota(jnp.int32, x.shape, 3)
    log_total = jnp.sum(jnp.where(slot == lane, log_row, 0.0), axis=3, keepdims=True)
    share = jnp.exp(log_total - jnp.max(log_total, axis=0, keepdims=True))
    heads = jnp.sum(share * x, axis=0) / jnp.sum(share, axis=0)
    packed = jnp.concatenate([heads[h, :GROUP] for h in range(KV_HEADS)], axis=0)
    out_ref[...] = jnp.broadcast_to(packed.astype(bf16)[None], out_ref.shape)


def merge(received):
    return pl.pallas_call(
        merge_kernel,
        in_specs=[VMEM],
        out_specs=VMEM,
        out_shape=jax.ShapeDtypeStruct((N_TP, HEADS, LANES), bf16),
        compiler_params=params(16),
        name="merge",
    )(received)


def output_kernel(*refs):
    x_ref, old_ref, *pieces, out_ref, wide, heads, late_parts = refs
    rep = lax.axis_index("rep")
    xx, zh = rep >> 1, rep & 1
    wide[...] = x_ref[...].astype(f32).reshape(wide.shape)
    for h in range(HEADS):
        kv = h // GROUP
        at = kv % 2 * HEADS + kv // 2 * GROUP + h % GROUP
        rows = [
            wide[pl.ds(at + el * HEADS // 2, HALF_TP, stride=2 * HEADS), :] for el in range(2)
        ]
        heads[:, h * HEAD_DIM : (h + 1) * HEAD_DIM] = jnp.concatenate(rows, axis=0).astype(bf16)
    contract_last = (((1,), (1,)), ((), ()))
    early_heads, late_heads = heads[:HALF_TP], heads[HALF_TP:]
    for n, piece in enumerate(pieces):
        place = ((xx + n // 2) & (N_X - 1)) * 2 + (zh ^ (n & 1))
        late_parts[place, :, :SHARD] = lax.dot_general(
            late_heads, piece[...], contract_last, preferred_element_type=f32
        )
    early = lax.dot_general(
        early_heads, old_ref[...], contract_last, preferred_element_type=f32
    )
    late = jnp.concatenate([late_parts[r, :, :SHARD] for r in range(N_REP)], axis=1)
    for r in range(ROWS):
        for el, total in enumerate((early, late)):
            out_ref[r, el * 2 : el * 2 + 2, :] = total[r * 2 : r * 2 + 2, :].astype(bf16)


def output(gathered, old_out, pieces):
    return pl.pallas_call(
        output_kernel,
        in_specs=[VMEM] * (2 + N_REP),
        out_specs=VMEM,
        out_shape=jax.ShapeDtypeStruct((ROWS, STEPS, FEAT), bf16),
        scratch_shapes=[
            pltpu.VMEM((N_TP * HEADS, LANES), f32),
            pltpu.VMEM((N_TP, D), bf16),
            pltpu.VMEM((N_REP, HALF_TP, LANES), f32),
        ],
        compiler_params=params(16),
        name="output",
    )(gathered, old_out.T, *pieces)


def rotation(cache_len):
    tp = lax.axis_index("tp")
    half_dim = HEAD_DIM // 2
    inverse_freq = ROPE_BASE ** (-jnp.arange(half_dim, dtype=f32) * 2.0 / HEAD_DIM)
    positions = cache_len[tp >> 2] + ((tp >> 1) & 1) + 2 * jnp.arange(2, dtype=jnp.int32)
    angles = positions.astype(f32)[:, None] * inverse_freq[None, :]
    cosine, sine = jnp.cos(angles), jnp.sin(angles)
    return (
        jnp.concatenate([cosine, cosine], axis=1),
        jnp.concatenate([-sine, sine], axis=1),
    )


def body(
    token_ids, cache_len, embed_table, norm_gain, old_qkv, old_out, new_qkv, new_out, kv_cache
):
    turn = [(r, r ^ 1) for r in range(N_REP)]
    ahead = [(r, (r + 2) % N_REP) for r in range(N_REP)]
    back = [(r, (r - 2) % N_REP) for r in range(N_REP)]
    other_qkv = lax.ppermute(new_qkv, "rep", turn)
    cosine, sine = rotation(cache_len)
    rows = gather_rows(token_ids, embed_table)
    rows, old_qkv = lax.optimization_barrier((rows, old_qkv))
    old_columns = take_old_columns(old_qkv)
    rows = lax.all_to_all(rows, "rep", 0, 0)
    rows, old_columns, cosine, sine = lax.optimization_barrier((rows, old_columns, cosine, sine))
    keep, send = project(rows, norm_gain, new_qkv, other_qkv, old_columns)
    arrived = lax.ppermute(send, "tp", [(t, t ^ 1) for t in range(N_TP)])
    summed = add(keep, arrived).reshape(DESTS, SUMS, LANES)
    groups = [
        [(x * 2 + zh) * N_TP + k * 2 + core for x in range(N_X) for k in range(HALF_TP)]
        for zh in range(2)
        for core in range(2)
    ]
    partials = lax.all_to_all(summed, ("rep", "tp"), 0, 0, axis_index_groups=groups)
    partials, own = lax.optimization_barrier((partials, new_out.T))
    other = lax.ppermute(own, "rep", turn)
    behind_own = lax.ppermute(own, "rep", ahead)
    front_own = lax.ppermute(own, "rep", back)
    projected = lax.all_to_all(finish(partials, cosine, sine, embed_table.T, embed_table.T, old_qkv), "tp", 0, 0)
    projected, other, behind_own = lax.optimization_barrier((projected, other, behind_own))
    far_own = lax.ppermute(behind_own, "rep", ahead)
    front_other = lax.ppermute(other, "rep", back)
    parts = lax.all_to_all(attend(cache_len, projected, kv_cache), "tp", 0, 0)
    parts, front_other, other = lax.optimization_barrier((parts, front_other, other))
    far_other = lax.ppermute(front_other, "rep", back)
    behind_other = lax.ppermute(other, "rep", ahead)
    heads = lax.all_to_all(merge(parts), "tp", 0, 0)
    pieces = (
        own,
        other,
        front_own,
        front_other,
        far_own,
        far_other,
        behind_own,
        behind_other,
    )
    return output(heads, old_out, pieces)


def solution(mesh):
    in_specs = (
        P(),
        P("rep"),
        P("rep", "tp"),
        P("tp"),
        P("tp", None),
        P(None, "tp"),
        P(("tp", "rep"), None),
        P(None, ("tp", "rep")),
        P("rep", "tp", None),
    )
    out_specs = P("rep", None, "tp")
    return jax.shard_map(body, mesh=mesh, in_specs=in_specs, out_specs=out_specs, check_vma=False)
```

```python
import functools

import jax
import jax.numpy as jnp
from jax import lax
from jax.experimental import pallas as pl
from jax.experimental.pallas import tpu as pltpu
from jax.sharding import PartitionSpec as P

D = 5120
HEADS = 40
KV_HEADS = 8
HEAD_DIM = 128
GROUP = HEADS // KV_HEADS
STEPS = 4
OLD_STEPS = 2
ROWS = 4
N_REP = 8
N_TP = 16
TOKENS = N_REP * ROWS * STEPS

NORM_EPSILON = 1e-06
ROPE_BASE = 1000000.0
MASK_VALUE = -1e30
SCORE_SCALE = 1.0 / HEAD_DIM**0.5

FEAT = D // N_TP
SHARD = FEAT // N_REP
LANES = 128
HALF_TP = N_TP // 2
N_X = 4
PART = FEAT // N_X
SLOTS = 8
USED = GROUP + 2
BLOCK = KV_HEADS * SLOTS
PER_CORE = KV_HEADS // 2
HALF_ROWS = PER_CORE * SLOTS
SUMS = HALF_ROWS + SLOTS
DESTS = N_X * HALF_TP
WIDE = 3 * LANES

f32 = jnp.float32
bf16 = jnp.bfloat16
MIB = 1 << 20

VMEM = pl.BlockSpec(memory_space=pltpu.VMEM)
SMEM = pl.BlockSpec(memory_space=pltpu.SMEM)
ANY = pl.BlockSpec(memory_space=pl.ANY)


def params(mib, grid=False):
    kwargs = dict(dimension_semantics=("arbitrary",) * grid) if grid else {}
    return pltpu.CompilerParams(vmem_limit_bytes=int(mib * MIB), **kwargs)

def gather_kernel(ids_ref, tail_ref, table_ref, out_ref, buf, cols, found, sems):
    window = table_ref.shape[1]
    tail_start = window // LANES * LANES
    start = lax.axis_index("rep") * window

    def local_id(i):
        step = ((i >> 5) & 1) * 2 + (i & 1)
        row = ((i >> 3) & 3) * 8 + (i >> 6) * 4 + ((i >> 1) & 3)
        return ids_ref[step, row] - start

    def note(i, count):
        local = local_id(i)
        found[count] = i
        return count + ((local >= 0) & (local < window)).astype(jnp.int32)

    count = lax.fori_loop(0, TOKENS, note, jnp.int32(0), unroll=32)

    def copy(j, local):
        base = pl.multiple_of((local >> 7) << 7, LANES)
        return pltpu.make_async_copy(
            table_ref.at[:, pl.ds(base, LANES)], buf.at[j], sems.at[j]
        )

    def begin(j, carry):
        local = local_id(found[j])

        @pl.when(local < tail_start)
        def _():
            copy(j, local).start()

        return carry

    lax.fori_loop(0, count, begin, 0)
    cols[...] = jnp.zeros_like(cols)
    lane = lax.broadcasted_iota(jnp.int32, (FEAT, LANES), 1)

    def place(i, local, block):
        shift = (i - local) & (LANES - 1)
        moved = pltpu.roll(block.astype(f32), shift, 1)
        cols[:FEAT] = jnp.where(lane == i, moved, cols[:FEAT])

    def end(j, carry):
        i = found[j]
        local = local_id(i)

        @pl.when(local < tail_start)
        def _():
            copy(j, local).wait()
            place(i, local, buf[j])

        @pl.when(local >= tail_start)
        def _():
            place(i, local, tail_ref[...])

        return carry

    lax.fori_loop(0, count, end, 0)
    rows = cols[...].T
    for zh in range(2):
        early = rows[zh * 64 : zh * 64 + DESTS]
        late = rows[zh * 64 + DESTS : zh * 64 + 2 * DESTS]
        tiles = [early[:, n * LANES : (n + 1) * LANES] for n in range(WIDE // LANES)]
        for xx in range(N_X):
            part = late[:, xx * PART : (xx + 1) * PART]
            blank = jnp.zeros((DESTS, LANES - PART), f32)
            block = jnp.concatenate(tiles + [jnp.concatenate([part, blank], axis=1)], axis=0)
            out_ref[xx * 2 + zh] = block.astype(bf16)


def gather_rows(token_ids, embed_table):
    table = embed_table.T
    tail = table.shape[1] // LANES
    return pl.pallas_call(
        gather_kernel,
        grid=(1,),
        in_specs=[SMEM, pl.BlockSpec((FEAT, LANES), lambda i: (0, tail)), ANY],
        out_specs=VMEM,
        out_shape=jax.ShapeDtypeStruct((N_REP, 4 * DESTS, LANES), bf16),
        scratch_shapes=[
            pltpu.VMEM((TOKENS, FEAT, LANES), bf16),
            pltpu.VMEM((WIDE, LANES), f32),
            pltpu.SMEM((TOKENS,), jnp.int32),
            pltpu.SemaphoreType.DMA((TOKENS,)),
        ],
        compiler_params=params(55),
        name="gather_rows",
    )(token_ids.T, table, table)


def old_columns_kernel(old_ref, out_ref, sems):
    xx = lax.axis_index("rep") >> 1
    copies = []
    for n, (first, width, to) in enumerate(
        (
            (0, 2 * GROUP, 0),
            (HEADS, 2, 2 * GROUP),
            (HEADS + KV_HEADS, 2, 2 * GROUP + 2),
        )
    ):
        at = pl.multiple_of((first + xx * width) * HEAD_DIM, HEAD_DIM)
        copies.append(
            pltpu.make_async_copy(
                old_ref.at[:, pl.ds(at, width * HEAD_DIM)],
                out_ref.at[:, pl.ds(to * HEAD_DIM, width * HEAD_DIM)],
                sems.at[n],
            )
        )
        copies[-1].start()
    for copy in copies:
        copy.wait()


def take_old_columns(old_qkv):
    shape = (FEAT, 2 * USED * HEAD_DIM)
    return pl.pallas_call(
        old_columns_kernel,
        in_specs=[ANY],
        out_specs=VMEM,
        out_shape=jax.ShapeDtypeStruct(shape, bf16),
        scratch_shapes=[pltpu.SemaphoreType.DMA((3,))],
        compiler_params=params(8),
        cost_estimate=pl.CostEstimate(
            flops=0, bytes_accessed=4 * shape[0] * shape[1], transcendentals=0
        ),
        name="take_old_columns",
    )(old_qkv)


def project_kernel(x_ref, gain_ref, new_ref, other_ref, old, keep_ref, send_ref):
    rep, core = lax.axis_index("rep"), lax.axis_index("tp") & 1
    xx, zh = rep >> 1, rep & 1
    embedded = jnp.sum(x_ref[...].astype(f32), axis=0)
    early = jnp.concatenate(
        [embedded[n * DESTS : (n + 1) * DESTS] for n in range(WIDE // LANES)], axis=1
    )
    late = embedded[3 * DESTS :]
    squares = [
        jnp.broadcast_to(jnp.sum(e * e, axis=1, keepdims=True), (DESTS, LANES))
        for e in (late, early)
    ]
    gain = gain_ref[...].astype(f32)
    part_gain = jnp.zeros((1, PART), f32)
    for i in range(N_X):
        part_gain = part_gain + jnp.where(xx == i, gain[:, i * PART : (i + 1) * PART], 0.0)
    early = (early[:, :FEAT] * gain).astype(bf16)
    late = (late[:, :PART] * part_gain).astype(bf16)
    first, second = late[:, :SHARD], late[:, SHARD:]
    late_own = jnp.where(zh == 0, first, second)
    late_other = jnp.where(zh == 0, second, first)

    def put(out_ref, group, slot, value):
        out_ref[pl.ds(group * SLOTS + slot, DESTS, stride=SUMS), :] = value

    for out_ref, side in ((keep_ref, core), (send_ref, 1 - core)):
        for j in range(PER_CORE):
            head = j * 2 + side
            starts = (
                (head * (GROUP * HEAD_DIM), GROUP, 0),
                (HEADS * HEAD_DIM + head * HEAD_DIM, 1, GROUP),
                ((HEADS + KV_HEADS) * HEAD_DIM + head * HEAD_DIM, 1, GROUP + 1),
            )
            for start, width, slot in starts:
                columns = pl.ds(pl.multiple_of(start, HEAD_DIM), width * HEAD_DIM)
                sums = jnp.dot(
                    late_own, new_ref[:, columns], preferred_element_type=f32
                ) + jnp.dot(late_other, other_ref[:, columns], preferred_element_type=f32)
                for g in range(width):
                    put(out_ref, j, slot + g, sums[:, g * HEAD_DIM : (g + 1) * HEAD_DIM])
            put(out_ref, j, SLOTS - 1, squares[0])
    sums = jnp.dot(early, old[...], preferred_element_type=f32)
    for slot in range(USED):
        at = (slot, slot + GROUP) if slot < GROUP else (slot * 2, slot * 2 + 1)
        both = [sums[:, a * HEAD_DIM : (a + 1) * HEAD_DIM] for a in at]
        put(keep_ref, PER_CORE, slot, jnp.where(core == 0, both[0], both[1]))
        put(send_ref, PER_CORE, slot, jnp.where(core == 0, both[1], both[0]))
    for out_ref in (keep_ref, send_ref):
        put(out_ref, PER_CORE, SLOTS - 1, squares[1])


def project(received, norm_gain, new_qkv, other_qkv, old_columns):
    out = jax.ShapeDtypeStruct((DESTS * SUMS, LANES), f32)
    return pl.pallas_call(
        project_kernel,
        in_specs=[VMEM] * 5,
        out_specs=[VMEM, VMEM],
        out_shape=[out, out],
        compiler_params=params(16),
        name="project",
    )(received, norm_gain.reshape(1, FEAT), new_qkv, other_qkv, old_columns)


def add_kernel(a_ref, b_ref, out_ref):
    out_ref[...] = a_ref[...] + b_ref[...]


def add(a, b):
    return pl.pallas_call(
        add_kernel,
        in_specs=[VMEM, VMEM],
        out_specs=VMEM,
        out_shape=jax.ShapeDtypeStruct(a.shape, a.dtype),
        compiler_params=params(16),
        name="add",
    )(a, b)


def finish_kernel(x_ref, cos_ref, sin_ref, *refs):
    out_ref = refs[-1]
    parts = x_ref[...].reshape(N_X, HALF_TP, SUMS, LANES)
    late = jnp.sum(jnp.sum(parts[:, :, :HALF_ROWS], axis=1), axis=0)
    early = jnp.sum(parts[:, :, HALF_ROWS:], axis=1)
    summed = jnp.concatenate([early.reshape(HALF_ROWS, LANES), late], axis=0).reshape(
        2, PER_CORE, SLOTS, LANES
    )
    squares = summed[:, :, SLOTS - 1 :, :]
    normed = summed / jnp.sqrt(squares / D + NORM_EPSILON)
    swapped = pltpu.roll(normed.reshape(BLOCK, LANES), HEAD_DIM // 2, 1).reshape(normed.shape)
    rotated = normed * cos_ref[...].reshape(2, 1, 1, LANES) + swapped * sin_ref[...].reshape(
        2, 1, 1, LANES
    )
    slot = lax.broadcasted_iota(jnp.int32, normed.shape, 2)
    result = jnp.where(slot <= GROUP, rotated, jnp.where(slot == GROUP + 1, normed, 0.0))
    out_ref[...] = jnp.broadcast_to(
        result.reshape(1, BLOCK, LANES).astype(bf16), out_ref.shape
    )


def finish(received, cosine, sine, *far):
    return pl.pallas_call(
        finish_kernel,
        in_specs=[VMEM, VMEM, VMEM] + [ANY] * len(far),
        out_specs=VMEM,
        out_shape=jax.ShapeDtypeStruct((N_TP, BLOCK, LANES), bf16),
        compiler_params=params(52),
        name="finish",
    )(received, cosine, sine, *far)


def attend_kernel(len_ref, q_ref, kv_ref, out_ref, scores_ref, weights_ref):
    row = pl.program_id(0)
    tp = lax.axis_index("tp")
    chunk = kv_ref.shape[1]
    value_at = KV_HEADS * HEAD_DIM
    count = STEPS * SLOTS
    blocks = [(row * 2 + s % 2) * 2 for s in range(STEPS)]
    rows_of = [slice(s // 2 * HALF_ROWS, (s // 2 + 1) * HALF_ROWS) for s in range(STEPS)]
    contract_last = (((1,), (1,)), ((), ()))
    by_core = [
        jnp.stack(
            [
                q_ref[b + core, r].astype(f32).reshape(PER_CORE, SLOTS, LANES)
                for b, r in zip(blocks, rows_of)
            ],
            axis=1,
        )
        for core in range(2)
    ]
    wide = jnp.stack(by_core, axis=1).reshape(KV_HEADS, count, LANES)
    queries = [wide[h].astype(bf16) for h in range(KV_HEADS)]
    shifted = [pltpu.roll(wide[h], count - 1, 0).astype(bf16) for h in range(KV_HEADS)]
    new = []
    for h in range(KV_HEADS):
        columns = slice(h * HEAD_DIM, (h + 1) * HEAD_DIM)
        scores_ref[h * count : (h + 1) * count, :] = lax.dot_general(
            queries[h], kv_ref[row, :, columns], contract_last, preferred_element_type=f32
        )
        new.append(
            lax.dot_general(queries[h], queries[h], contract_last, preferred_element_type=f32)
        )
    valid = len_ref[row] - tp * chunk
    shape = scores_ref.shape
    position = lax.broadcasted_iota(jnp.int32, shape, 1)
    scores = jnp.where(position < valid, scores_ref[...] * SCORE_SCALE, MASK_VALUE)
    from_step = (lax.broadcasted_iota(jnp.int32, (shape[0], count), 0) >> 3) & (STEPS - 1)
    column = lax.broadcasted_iota(jnp.int32, (shape[0], count), 1)
    new_mask = ((column & (SLOTS - 1)) == GROUP) & ((column >> 3) <= from_step) & (tp == 0)
    scores_new = jnp.where(new_mask, jnp.concatenate(new, axis=0) * SCORE_SCALE, MASK_VALUE)
    peak = jnp.maximum(
        jnp.max(scores, axis=1, keepdims=True), jnp.max(scores_new, axis=1, keepdims=True)
    )
    weights = jnp.exp(scores - peak).astype(bf16)
    weights_new = jnp.exp(scores_new - peak).astype(bf16)
    weights_ref[...] = weights
    total = jnp.sum(weights.astype(f32), axis=1, keepdims=True) + jnp.sum(
        weights_new.astype(f32), axis=1, keepdims=True
    )
    numerator = []
    for h in range(KV_HEADS):
        columns = slice(value_at + h * HEAD_DIM, value_at + (h + 1) * HEAD_DIM)
        rows = slice(h * count, (h + 1) * count)
        numerator.append(
            jnp.dot(weights_ref[rows, :], kv_ref[row, :, columns], preferred_element_type=f32)
            + jnp.dot(weights_new[rows], shifted[h], preferred_element_type=f32)
        )
    grouped = (KV_HEADS, STEPS, SLOTS, LANES)
    part = (jnp.concatenate(numerator, axis=0) / total).reshape(grouped)
    slot = lax.broadcasted_iota(jnp.int32, grouped, 2)
    diagonal = slot == lax.broadcasted_iota(jnp.int32, grouped, 3)
    log_total = jnp.broadcast_to(peak + jnp.log(total), (shape[0], LANES)).reshape(grouped)
    log_row = jnp.sum(jnp.where(diagonal, log_total, 0.0), axis=2, keepdims=True)
    high = log_row.astype(bf16).astype(f32)
    middle = (log_row - high).astype(bf16).astype(f32)
    low = log_row - high - middle
    part = jnp.where(
        slot < GROUP,
        part,
        jnp.where(slot == GROUP, high, jnp.where(slot == GROUP + 1, middle, low)),
    )
    by_core = part.reshape(PER_CORE, 2, STEPS, SLOTS, LANES)
    for core in range(2):
        for s, (b, r) in enumerate(zip(blocks, rows_of)):
            out_ref[b + core, r] = by_core[:, core, s].reshape(HALF_ROWS, LANES).astype(bf16)


def attend(cache_len, gathered, kv_cache):
    chunk = kv_cache.shape[1]
    whole = pl.BlockSpec((N_TP, BLOCK, LANES), lambda r: (0, 0, 0))
    lines = KV_HEADS * STEPS * SLOTS
    return pl.pallas_call(
        attend_kernel,
        grid=(ROWS,),
        in_specs=[
            SMEM,
            whole,
            VMEM,
        ],
        out_specs=whole,
        out_shape=jax.ShapeDtypeStruct((N_TP, BLOCK, LANES), bf16),
        scratch_shapes=[pltpu.VMEM((lines, chunk), f32), pltpu.VMEM((lines, chunk), bf16)],
        compiler_params=params(16, 1),
        name="attend",
    )(cache_len, gathered, kv_cache)


def merge_kernel(x_ref, out_ref):
    x = x_ref[...].astype(f32).reshape(N_TP, KV_HEADS, SLOTS, LANES)
    log_row = jnp.sum(x[:, :, GROUP:, :], axis=2, keepdims=True)
    slot = lax.broadcasted_iota(jnp.int32, x.shape, 2)
    lane = lax.broadcasted_iota(jnp.int32, x.shape, 3)
    log_total = jnp.sum(jnp.where(slot == lane, log_row, 0.0), axis=3, keepdims=True)
    share = jnp.exp(log_total - jnp.max(log_total, axis=0, keepdims=True))
    heads = jnp.sum(share * x, axis=0) / jnp.sum(share, axis=0)
    packed = jnp.concatenate([heads[h, :GROUP] for h in range(KV_HEADS)], axis=0)
    out_ref[...] = jnp.broadcast_to(packed.astype(bf16)[None], out_ref.shape)


def merge(received):
    return pl.pallas_call(
        merge_kernel,
        in_specs=[VMEM],
        out_specs=VMEM,
        out_shape=jax.ShapeDtypeStruct((N_TP, HEADS, LANES), bf16),
        compiler_params=params(16),
        name="merge",
    )(received)


def output_kernel(*refs):
    x_ref, old_ref, *pieces, out_ref, wide, heads, late_parts = refs
    rep = lax.axis_index("rep")
    xx, zh = rep >> 1, rep & 1
    wide[...] = x_ref[...].astype(f32).reshape(wide.shape)
    for h in range(HEADS):
        kv = h // GROUP
        at = kv % 2 * HEADS + kv // 2 * GROUP + h % GROUP
        rows = [
            wide[pl.ds(at + el * HEADS // 2, HALF_TP, stride=2 * HEADS), :] for el in range(2)
        ]
        heads[:, h * HEAD_DIM : (h + 1) * HEAD_DIM] = jnp.concatenate(rows, axis=0).astype(bf16)
    contract_last = (((1,), (1,)), ((), ()))
    early_heads, late_heads = heads[:HALF_TP], heads[HALF_TP:]
    for n, piece in enumerate(pieces):
        place = ((xx + n // 2) & (N_X - 1)) * 2 + (zh ^ (n & 1))
        late_parts[place, :, :SHARD] = lax.dot_general(
            late_heads, piece[...], contract_last, preferred_element_type=f32
        )
    early = lax.dot_general(
        early_heads, old_ref[...], contract_last, preferred_element_type=f32
    )
    late = jnp.concatenate([late_parts[r, :, :SHARD] for r in range(N_REP)], axis=1)
    for r in range(ROWS):
        for el, total in enumerate((early, late)):
            out_ref[r, el * 2 : el * 2 + 2, :] = total[r * 2 : r * 2 + 2, :].astype(bf16)


def output(gathered, old_out, pieces):
    return pl.pallas_call(
        output_kernel,
        in_specs=[VMEM] * (2 + N_REP),
        out_specs=VMEM,
        out_shape=jax.ShapeDtypeStruct((ROWS, STEPS, FEAT), bf16),
        scratch_shapes=[
            pltpu.VMEM((N_TP * HEADS, LANES), f32),
            pltpu.VMEM((N_TP, D), bf16),
            pltpu.VMEM((N_REP, HALF_TP, LANES), f32),
        ],
        compiler_params=params(16),
        name="output",
    )(gathered, old_out.T, *pieces)


def rotation(cache_len):
    tp = lax.axis_index("tp")
    half_dim = HEAD_DIM // 2
    inverse_freq = ROPE_BASE ** (-jnp.arange(half_dim, dtype=f32) * 2.0 / HEAD_DIM)
    positions = cache_len[tp >> 2] + ((tp >> 1) & 1) + 2 * jnp.arange(2, dtype=jnp.int32)
    angles = positions.astype(f32)[:, None] * inverse_freq[None, :]
    cosine, sine = jnp.cos(angles), jnp.sin(angles)
    return (
        jnp.concatenate([cosine, cosine], axis=1),
        jnp.concatenate([-sine, sine], axis=1),
    )


def body(
    token_ids, cache_len, embed_table, norm_gain, old_qkv, old_out, new_qkv, new_out, kv_cache
):
    turn = [(r, r ^ 1) for r in range(N_REP)]
    ahead = [(r, (r + 2) % N_REP) for r in range(N_REP)]
    back = [(r, (r - 2) % N_REP) for r in range(N_REP)]
    other_qkv = lax.ppermute(new_qkv, "rep", turn)
    cosine, sine = rotation(cache_len)
    rows = gather_rows(token_ids, embed_table)
    rows, old_qkv = lax.optimization_barrier((rows, old_qkv))
    old_columns = take_old_columns(old_qkv)
    rows = lax.all_to_all(rows, "rep", 0, 0)
    rows, old_columns, cosine, sine = lax.optimization_barrier((rows, old_columns, cosine, sine))
    keep, send = project(rows, norm_gain, new_qkv, other_qkv, old_columns)
    arrived = lax.ppermute(send, "tp", [(t, t ^ 1) for t in range(N_TP)])
    summed = add(keep, arrived).reshape(DESTS, SUMS, LANES)
    groups = [
        [(x * 2 + zh) * N_TP + k * 2 + core for x in range(N_X) for k in range(HALF_TP)]
        for zh in range(2)
        for core in range(2)
    ]
    partials = lax.all_to_all(summed, ("rep", "tp"), 0, 0, axis_index_groups=groups)
    partials, own = lax.optimization_barrier((partials, new_out.T))
    other = lax.ppermute(own, "rep", turn)
    behind_own = lax.ppermute(own, "rep", ahead)
    front_own = lax.ppermute(own, "rep", back)
    projected = lax.all_to_all(finish(partials, cosine, sine, embed_table.T, embed_table.T, old_qkv), "tp", 0, 0)
    projected, other, behind_own, front_own = lax.optimization_barrier(
        (projected, other, behind_own, front_own)
    )
    far_own = lax.ppermute(behind_own, "rep", ahead)
    front_other = lax.ppermute(other, "rep", back)
    parts = lax.all_to_all(attend(cache_len, projected, kv_cache), "tp", 0, 0)
    parts, front_other, other, far_own = lax.optimization_barrier(
        (parts, front_other, other, far_own)
    )
    far_other = lax.ppermute(front_other, "rep", back)
    behind_other = lax.ppermute(other, "rep", ahead)
    heads = lax.all_to_all(merge(parts), "tp", 0, 0)
    pieces = (
        own,
        other,
        front_own,
        front_other,
        far_own,
        far_other,
        behind_own,
        behind_other,
    )
    return output(heads, old_out, pieces)


def solution(mesh):
    in_specs = (
        P(),
        P("rep"),
        P("rep", "tp"),
        P("tp"),
        P("tp", None),
        P(None, "tp"),
        P(("tp", "rep"), None),
        P(None, ("tp", "rep")),
        P("rep", "tp", None),
    )
    out_specs = P("rep", None, "tp")
    return jax.shard_map(body, mesh=mesh, in_specs=in_specs, out_specs=out_specs, check_vma=False)
```

```python
import functools

import jax
import jax.numpy as jnp
from jax import lax
from jax.experimental import pallas as pl
from jax.experimental.pallas import tpu as pltpu
from jax.sharding import PartitionSpec as P

D = 5120
HEADS = 40
KV_HEADS = 8
HEAD_DIM = 128
GROUP = HEADS // KV_HEADS
STEPS = 4
OLD_STEPS = 2
ROWS = 4
N_REP = 8
N_TP = 16
TOKENS = N_REP * ROWS * STEPS

NORM_EPSILON = 1e-06
ROPE_BASE = 1000000.0
MASK_VALUE = -1e30
SCORE_SCALE = 1.0 / HEAD_DIM**0.5

FEAT = D // N_TP
SHARD = FEAT // N_REP
LANES = 128
HALF_TP = N_TP // 2
N_X = 4
PART = FEAT // N_X
SLOTS = 8
USED = GROUP + 2
BLOCK = KV_HEADS * SLOTS
PER_CORE = KV_HEADS // 2
HALF_ROWS = PER_CORE * SLOTS
SUMS = HALF_ROWS + SLOTS
DESTS = N_X * HALF_TP
WIDE = 3 * LANES

f32 = jnp.float32
bf16 = jnp.bfloat16
MIB = 1 << 20

VMEM = pl.BlockSpec(memory_space=pltpu.VMEM)
SMEM = pl.BlockSpec(memory_space=pltpu.SMEM)
ANY = pl.BlockSpec(memory_space=pl.ANY)


def params(mib, grid=False):
    kwargs = dict(dimension_semantics=("arbitrary",) * grid) if grid else {}
    return pltpu.CompilerParams(vmem_limit_bytes=int(mib * MIB), **kwargs)

def gather_kernel(ids_ref, tail_ref, table_ref, out_ref, buf, cols, found, places, sems):
    window = table_ref.shape[1]
    tail_start = window // LANES * LANES
    start = lax.axis_index("rep") * window

    count = jnp.int32(0)
    for i in range(TOKENS):
        step = ((i >> 5) & 1) * 2 + (i & 1)
        row = ((i >> 3) & 3) * 8 + (i >> 6) * 4 + ((i >> 1) & 3)
        local = ids_ref[step, row] - start
        found[count] = i
        places[count] = local
        count = count + ((local >= 0) & (local < window)).astype(jnp.int32)

    def copy(j, local):
        base = pl.multiple_of((local >> 7) << 7, LANES)
        return pltpu.make_async_copy(
            table_ref.at[:, pl.ds(base, LANES)], buf.at[j], sems.at[j]
        )

    def begin(j, carry):
        local = places[j]

        @pl.when(local < tail_start)
        def _():
            copy(j, local).start()

        return carry

    lax.fori_loop(0, count, begin, 0)
    cols[...] = jnp.zeros_like(cols)
    lane = lax.broadcasted_iota(jnp.int32, (FEAT, LANES), 1)

    def place(i, local, block):
        shift = (i - local) & (LANES - 1)
        moved = pltpu.roll(block.astype(f32), shift, 1)
        cols[:FEAT] = jnp.where(lane == i, moved, cols[:FEAT])

    def end(j, carry):
        i, local = found[j], places[j]

        @pl.when(local < tail_start)
        def _():
            copy(j, local).wait()
            place(i, local, buf[j])

        @pl.when(local >= tail_start)
        def _():
            place(i, local, tail_ref[...])

        return carry

    lax.fori_loop(0, count, end, 0)
    rows = cols[...].T
    for zh in range(2):
        early = rows[zh * 64 : zh * 64 + DESTS]
        late = rows[zh * 64 + DESTS : zh * 64 + 2 * DESTS]
        tiles = [early[:, n * LANES : (n + 1) * LANES] for n in range(WIDE // LANES)]
        for xx in range(N_X):
            part = late[:, xx * PART : (xx + 1) * PART]
            blank = jnp.zeros((DESTS, LANES - PART), f32)
            block = jnp.concatenate(tiles + [jnp.concatenate([part, blank], axis=1)], axis=0)
            out_ref[xx * 2 + zh] = block.astype(bf16)


def gather_rows(token_ids, embed_table):
    table = embed_table.T
    tail = table.shape[1] // LANES
    return pl.pallas_call(
        gather_kernel,
        grid=(1,),
        in_specs=[SMEM, pl.BlockSpec((FEAT, LANES), lambda i: (0, tail)), ANY],
        out_specs=VMEM,
        out_shape=jax.ShapeDtypeStruct((N_REP, 4 * DESTS, LANES), bf16),
        scratch_shapes=[
            pltpu.VMEM((TOKENS, FEAT, LANES), bf16),
            pltpu.VMEM((WIDE, LANES), f32),
            pltpu.SMEM((TOKENS,), jnp.int32),
            pltpu.SMEM((TOKENS,), jnp.int32),
            pltpu.SemaphoreType.DMA((TOKENS,)),
        ],
        compiler_params=params(55),
        name="gather_rows",
    )(token_ids.T, table, table)


def old_columns_kernel(old_ref, out_ref, sems):
    xx = lax.axis_index("rep") >> 1
    copies = []
    for n, (first, width, to) in enumerate(
        (
            (0, 2 * GROUP, 0),
            (HEADS, 2, 2 * GROUP),
            (HEADS + KV_HEADS, 2, 2 * GROUP + 2),
        )
    ):
        at = pl.multiple_of((first + xx * width) * HEAD_DIM, HEAD_DIM)
        copies.append(
            pltpu.make_async_copy(
                old_ref.at[:, pl.ds(at, width * HEAD_DIM)],
                out_ref.at[:, pl.ds(to * HEAD_DIM, width * HEAD_DIM)],
                sems.at[n],
            )
        )
        copies[-1].start()
    for copy in copies:
        copy.wait()


def take_old_columns(old_qkv):
    shape = (FEAT, 2 * USED * HEAD_DIM)
    return pl.pallas_call(
        old_columns_kernel,
        in_specs=[ANY],
        out_specs=VMEM,
        out_shape=jax.ShapeDtypeStruct(shape, bf16),
        scratch_shapes=[pltpu.SemaphoreType.DMA((3,))],
        compiler_params=params(8),
        cost_estimate=pl.CostEstimate(
            flops=0, bytes_accessed=4 * shape[0] * shape[1], transcendentals=0
        ),
        name="take_old_columns",
    )(old_qkv)


def project_kernel(x_ref, gain_ref, new_ref, other_ref, old, keep_ref, send_ref):
    rep, core = lax.axis_index("rep"), lax.axis_index("tp") & 1
    xx, zh = rep >> 1, rep & 1
    embedded = jnp.sum(x_ref[...].astype(f32), axis=0)
    early = jnp.concatenate(
        [embedded[n * DESTS : (n + 1) * DESTS] for n in range(WIDE // LANES)], axis=1
    )
    late = embedded[3 * DESTS :]
    squares = [
        jnp.broadcast_to(jnp.sum(e * e, axis=1, keepdims=True), (DESTS, LANES))
        for e in (late, early)
    ]
    gain = gain_ref[...].astype(f32)
    part_gain = jnp.zeros((1, PART), f32)
    for i in range(N_X):
        part_gain = part_gain + jnp.where(xx == i, gain[:, i * PART : (i + 1) * PART], 0.0)
    early = (early[:, :FEAT] * gain).astype(bf16)
    late = (late[:, :PART] * part_gain).astype(bf16)
    first, second = late[:, :SHARD], late[:, SHARD:]
    late_own = jnp.where(zh == 0, first, second)
    late_other = jnp.where(zh == 0, second, first)

    def put(out_ref, group, slot, value):
        out_ref[pl.ds(group * SLOTS + slot, DESTS, stride=SUMS), :] = value

    for out_ref, side in ((keep_ref, core), (send_ref, 1 - core)):
        for j in range(PER_CORE):
            head = j * 2 + side
            starts = (
                (head * (GROUP * HEAD_DIM), GROUP, 0),
                (HEADS * HEAD_DIM + head * HEAD_DIM, 1, GROUP),
                ((HEADS + KV_HEADS) * HEAD_DIM + head * HEAD_DIM, 1, GROUP + 1),
            )
            for start, width, slot in starts:
                columns = pl.ds(pl.multiple_of(start, HEAD_DIM), width * HEAD_DIM)
                sums = jnp.dot(
                    late_own, new_ref[:, columns], preferred_element_type=f32
                ) + jnp.dot(late_other, other_ref[:, columns], preferred_element_type=f32)
                for g in range(width):
                    put(out_ref, j, slot + g, sums[:, g * HEAD_DIM : (g + 1) * HEAD_DIM])
            put(out_ref, j, SLOTS - 1, squares[0])
    sums = jnp.dot(early, old[...], preferred_element_type=f32)
    for slot in range(USED):
        at = (slot, slot + GROUP) if slot < GROUP else (slot * 2, slot * 2 + 1)
        both = [sums[:, a * HEAD_DIM : (a + 1) * HEAD_DIM] for a in at]
        put(keep_ref, PER_CORE, slot, jnp.where(core == 0, both[0], both[1]))
        put(send_ref, PER_CORE, slot, jnp.where(core == 0, both[1], both[0]))
    for out_ref in (keep_ref, send_ref):
        put(out_ref, PER_CORE, SLOTS - 1, squares[1])


def project(received, norm_gain, new_qkv, other_qkv, old_columns):
    out = jax.ShapeDtypeStruct((DESTS * SUMS, LANES), f32)
    return pl.pallas_call(
        project_kernel,
        in_specs=[VMEM] * 5,
        out_specs=[VMEM, VMEM],
        out_shape=[out, out],
        compiler_params=params(16),
        name="project",
    )(received, norm_gain.reshape(1, FEAT), new_qkv, other_qkv, old_columns)


def add_kernel(a_ref, b_ref, out_ref):
    out_ref[...] = a_ref[...] + b_ref[...]


def add(a, b):
    return pl.pallas_call(
        add_kernel,
        in_specs=[VMEM, VMEM],
        out_specs=VMEM,
        out_shape=jax.ShapeDtypeStruct(a.shape, a.dtype),
        compiler_params=params(16),
        name="add",
    )(a, b)


def finish_kernel(x_ref, cos_ref, sin_ref, *refs):
    out_ref = refs[-1]
    parts = x_ref[...].reshape(N_X, HALF_TP, SUMS, LANES)
    late = jnp.sum(jnp.sum(parts[:, :, :HALF_ROWS], axis=1), axis=0)
    early = jnp.sum(parts[:, :, HALF_ROWS:], axis=1)
    summed = jnp.concatenate([early.reshape(HALF_ROWS, LANES), late], axis=0).reshape(
        2, PER_CORE, SLOTS, LANES
    )
    squares = summed[:, :, SLOTS - 1 :, :]
    normed = summed / jnp.sqrt(squares / D + NORM_EPSILON)
    swapped = pltpu.roll(normed.reshape(BLOCK, LANES), HEAD_DIM // 2, 1).reshape(normed.shape)
    rotated = normed * cos_ref[...].reshape(2, 1, 1, LANES) + swapped * sin_ref[...].reshape(
        2, 1, 1, LANES
    )
    slot = lax.broadcasted_iota(jnp.int32, normed.shape, 2)
    result = jnp.where(slot <= GROUP, rotated, jnp.where(slot == GROUP + 1, normed, 0.0))
    out_ref[...] = jnp.broadcast_to(
        result.reshape(1, BLOCK, LANES).astype(bf16), out_ref.shape
    )


def finish(received, cosine, sine, *far):
    return pl.pallas_call(
        finish_kernel,
        in_specs=[VMEM, VMEM, VMEM] + [ANY] * len(far),
        out_specs=VMEM,
        out_shape=jax.ShapeDtypeStruct((N_TP, BLOCK, LANES), bf16),
        compiler_params=params(52),
        name="finish",
    )(received, cosine, sine, *far)


def attend_kernel(len_ref, q_ref, kv_ref, out_ref, scores_ref, weights_ref):
    row = pl.program_id(0)
    tp = lax.axis_index("tp")
    chunk = kv_ref.shape[1]
    value_at = KV_HEADS * HEAD_DIM
    count = STEPS * SLOTS
    blocks = [(row * 2 + s % 2) * 2 for s in range(STEPS)]
    rows_of = [slice(s // 2 * HALF_ROWS, (s // 2 + 1) * HALF_ROWS) for s in range(STEPS)]
    contract_last = (((1,), (1,)), ((), ()))
    by_core = [
        jnp.stack(
            [
                q_ref[b + core, r].astype(f32).reshape(PER_CORE, SLOTS, LANES)
                for b, r in zip(blocks, rows_of)
            ],
            axis=1,
        )
        for core in range(2)
    ]
    wide = jnp.stack(by_core, axis=1).reshape(KV_HEADS, count, LANES)
    queries = [wide[h].astype(bf16) for h in range(KV_HEADS)]
    shifted = [pltpu.roll(wide[h], count - 1, 0).astype(bf16) for h in range(KV_HEADS)]
    new = []
    for h in range(KV_HEADS):
        columns = slice(h * HEAD_DIM, (h + 1) * HEAD_DIM)
        scores_ref[h * count : (h + 1) * count, :] = lax.dot_general(
            queries[h], kv_ref[row, :, columns], contract_last, preferred_element_type=f32
        )
        new.append(
            lax.dot_general(queries[h], queries[h], contract_last, preferred_element_type=f32)
        )
    valid = len_ref[row] - tp * chunk
    shape = scores_ref.shape
    position = lax.broadcasted_iota(jnp.int32, shape, 1)
    scores = jnp.where(position < valid, scores_ref[...] * SCORE_SCALE, MASK_VALUE)
    from_step = (lax.broadcasted_iota(jnp.int32, (shape[0], count), 0) >> 3) & (STEPS - 1)
    column = lax.broadcasted_iota(jnp.int32, (shape[0], count), 1)
    new_mask = ((column & (SLOTS - 1)) == GROUP) & ((column >> 3) <= from_step) & (tp == 0)
    scores_new = jnp.where(new_mask, jnp.concatenate(new, axis=0) * SCORE_SCALE, MASK_VALUE)
    peak = jnp.maximum(
        jnp.max(scores, axis=1, keepdims=True), jnp.max(scores_new, axis=1, keepdims=True)
    )
    weights = jnp.exp(scores - peak).astype(bf16)
    weights_new = jnp.exp(scores_new - peak).astype(bf16)
    weights_ref[...] = weights
    total = jnp.sum(weights.astype(f32), axis=1, keepdims=True) + jnp.sum(
        weights_new.astype(f32), axis=1, keepdims=True
    )
    numerator = []
    for h in range(KV_HEADS):
        columns = slice(value_at + h * HEAD_DIM, value_at + (h + 1) * HEAD_DIM)
        rows = slice(h * count, (h + 1) * count)
        numerator.append(
            jnp.dot(weights_ref[rows, :], kv_ref[row, :, columns], preferred_element_type=f32)
            + jnp.dot(weights_new[rows], shifted[h], preferred_element_type=f32)
        )
    grouped = (KV_HEADS, STEPS, SLOTS, LANES)
    part = (jnp.concatenate(numerator, axis=0) / total).reshape(grouped)
    slot = lax.broadcasted_iota(jnp.int32, grouped, 2)
    diagonal = slot == lax.broadcasted_iota(jnp.int32, grouped, 3)
    log_total = jnp.broadcast_to(peak + jnp.log(total), (shape[0], LANES)).reshape(grouped)
    log_row = jnp.sum(jnp.where(diagonal, log_total, 0.0), axis=2, keepdims=True)
    high = log_row.astype(bf16).astype(f32)
    middle = (log_row - high).astype(bf16).astype(f32)
    low = log_row - high - middle
    part = jnp.where(
        slot < GROUP,
        part,
        jnp.where(slot == GROUP, high, jnp.where(slot == GROUP + 1, middle, low)),
    )
    by_core = part.reshape(PER_CORE, 2, STEPS, SLOTS, LANES)
    for core in range(2):
        for s, (b, r) in enumerate(zip(blocks, rows_of)):
            out_ref[b + core, r] = by_core[:, core, s].reshape(HALF_ROWS, LANES).astype(bf16)


def attend(cache_len, gathered, kv_cache):
    chunk = kv_cache.shape[1]
    whole = pl.BlockSpec((N_TP, BLOCK, LANES), lambda r: (0, 0, 0))
    lines = KV_HEADS * STEPS * SLOTS
    return pl.pallas_call(
        attend_kernel,
        grid=(ROWS,),
        in_specs=[
            SMEM,
            whole,
            VMEM,
        ],
        out_specs=whole,
        out_shape=jax.ShapeDtypeStruct((N_TP, BLOCK, LANES), bf16),
        scratch_shapes=[pltpu.VMEM((lines, chunk), f32), pltpu.VMEM((lines, chunk), bf16)],
        compiler_params=params(16, 1),
        name="attend",
    )(cache_len, gathered, kv_cache)


def merge_kernel(x_ref, out_ref):
    x = x_ref[...].astype(f32).reshape(N_TP, KV_HEADS, SLOTS, LANES)
    log_row = jnp.sum(x[:, :, GROUP:, :], axis=2, keepdims=True)
    slot = lax.broadcasted_iota(jnp.int32, x.shape, 2)
    lane = lax.broadcasted_iota(jnp.int32, x.shape, 3)
    log_total = jnp.sum(jnp.where(slot == lane, log_row, 0.0), axis=3, keepdims=True)
    share = jnp.exp(log_total - jnp.max(log_total, axis=0, keepdims=True))
    heads = jnp.sum(share * x, axis=0) / jnp.sum(share, axis=0)
    packed = jnp.concatenate([heads[h, :GROUP] for h in range(KV_HEADS)], axis=0)
    out_ref[...] = jnp.broadcast_to(packed.astype(bf16)[None], out_ref.shape)


def merge(received):
    return pl.pallas_call(
        merge_kernel,
        in_specs=[VMEM],
        out_specs=VMEM,
        out_shape=jax.ShapeDtypeStruct((N_TP, HEADS, LANES), bf16),
        compiler_params=params(16),
        name="merge",
    )(received)


def output_kernel(*refs):
    x_ref, old_ref, *pieces, out_ref, wide, heads, late_parts = refs
    rep = lax.axis_index("rep")
    xx, zh = rep >> 1, rep & 1
    wide[...] = x_ref[...].astype(f32).reshape(wide.shape)
    for h in range(HEADS):
        kv = h // GROUP
        at = kv % 2 * HEADS + kv // 2 * GROUP + h % GROUP
        rows = [
            wide[pl.ds(at + el * HEADS // 2, HALF_TP, stride=2 * HEADS), :] for el in range(2)
        ]
        heads[:, h * HEAD_DIM : (h + 1) * HEAD_DIM] = jnp.concatenate(rows, axis=0).astype(bf16)
    contract_last = (((1,), (1,)), ((), ()))
    early_heads, late_heads = heads[:HALF_TP], heads[HALF_TP:]
    for n, piece in enumerate(pieces):
        place = ((xx + n // 2) & (N_X - 1)) * 2 + (zh ^ (n & 1))
        late_parts[place, :, :SHARD] = lax.dot_general(
            late_heads, piece[...], contract_last, preferred_element_type=f32
        )
    early = lax.dot_general(
        early_heads, old_ref[...], contract_last, preferred_element_type=f32
    )
    late = jnp.concatenate([late_parts[r, :, :SHARD] for r in range(N_REP)], axis=1)
    for r in range(ROWS):
        for el, total in enumerate((early, late)):
            out_ref[r, el * 2 : el * 2 + 2, :] = total[r * 2 : r * 2 + 2, :].astype(bf16)


def output(gathered, old_out, pieces):
    return pl.pallas_call(
        output_kernel,
        in_specs=[VMEM] * (2 + N_REP),
        out_specs=VMEM,
        out_shape=jax.ShapeDtypeStruct((ROWS, STEPS, FEAT), bf16),
        scratch_shapes=[
            pltpu.VMEM((N_TP * HEADS, LANES), f32),
            pltpu.VMEM((N_TP, D), bf16),
            pltpu.VMEM((N_REP, HALF_TP, LANES), f32),
        ],
        compiler_params=params(16),
        name="output",
    )(gathered, old_out.T, *pieces)


def rotation(cache_len):
    tp = lax.axis_index("tp")
    half_dim = HEAD_DIM // 2
    inverse_freq = ROPE_BASE ** (-jnp.arange(half_dim, dtype=f32) * 2.0 / HEAD_DIM)
    positions = cache_len[tp >> 2] + ((tp >> 1) & 1) + 2 * jnp.arange(2, dtype=jnp.int32)
    angles = positions.astype(f32)[:, None] * inverse_freq[None, :]
    cosine, sine = jnp.cos(angles), jnp.sin(angles)
    return (
        jnp.concatenate([cosine, cosine], axis=1),
        jnp.concatenate([-sine, sine], axis=1),
    )


def body(
    token_ids, cache_len, embed_table, norm_gain, old_qkv, old_out, new_qkv, new_out, kv_cache
):
    turn = [(r, r ^ 1) for r in range(N_REP)]
    ahead = [(r, (r + 2) % N_REP) for r in range(N_REP)]
    back = [(r, (r - 2) % N_REP) for r in range(N_REP)]
    other_qkv = lax.ppermute(new_qkv, "rep", turn)
    cosine, sine = rotation(cache_len)
    rows = gather_rows(token_ids, embed_table)
    rows, old_qkv = lax.optimization_barrier((rows, old_qkv))
    old_columns = take_old_columns(old_qkv)
    rows = lax.all_to_all(rows, "rep", 0, 0)
    rows, old_columns, cosine, sine = lax.optimization_barrier((rows, old_columns, cosine, sine))
    keep, send = project(rows, norm_gain, new_qkv, other_qkv, old_columns)
    arrived = lax.ppermute(send, "tp", [(t, t ^ 1) for t in range(N_TP)])
    summed = add(keep, arrived).reshape(DESTS, SUMS, LANES)
    groups = [
        [(x * 2 + zh) * N_TP + k * 2 + core for x in range(N_X) for k in range(HALF_TP)]
        for zh in range(2)
        for core in range(2)
    ]
    partials = lax.all_to_all(summed, ("rep", "tp"), 0, 0, axis_index_groups=groups)
    partials, own = lax.optimization_barrier((partials, new_out.T))
    other = lax.ppermute(own, "rep", turn)
    behind_own = lax.ppermute(own, "rep", ahead)
    front_own = lax.ppermute(own, "rep", back)
    projected = lax.all_to_all(finish(partials, cosine, sine, embed_table.T, embed_table.T, old_qkv), "tp", 0, 0)
    projected, other, behind_own, front_own = lax.optimization_barrier(
        (projected, other, behind_own, front_own)
    )
    far_own = lax.ppermute(behind_own, "rep", ahead)
    front_other = lax.ppermute(other, "rep", back)
    parts = lax.all_to_all(attend(cache_len, projected, kv_cache), "tp", 0, 0)
    parts, front_other, other, far_own = lax.optimization_barrier(
        (parts, front_other, other, far_own)
    )
    far_other = lax.ppermute(front_other, "rep", back)
    behind_other = lax.ppermute(other, "rep", ahead)
    heads = lax.all_to_all(merge(parts), "tp", 0, 0)
    pieces = (
        own,
        other,
        front_own,
        front_other,
        far_own,
        far_other,
        behind_own,
        behind_other,
    )
    return output(heads, old_out, pieces)


def solution(mesh):
    in_specs = (
        P(),
        P("rep"),
        P("rep", "tp"),
        P("tp"),
        P("tp", None),
        P(None, "tp"),
        P(("tp", "rep"), None),
        P(None, ("tp", "rep")),
        P("rep", "tp", None),
    )
    out_specs = P("rep", None, "tp")
    return jax.shard_map(body, mesh=mesh, in_specs=in_specs, out_specs=out_specs, check_vma=False)
```

```python
import functools

import jax
import jax.numpy as jnp
from jax import lax
from jax.experimental import pallas as pl
from jax.experimental.pallas import tpu as pltpu
from jax.sharding import PartitionSpec as P

D = 5120
HEADS = 40
KV_HEADS = 8
HEAD_DIM = 128
GROUP = HEADS // KV_HEADS
STEPS = 4
OLD_STEPS = 2
ROWS = 4
N_REP = 8
N_TP = 16
TOKENS = N_REP * ROWS * STEPS

NORM_EPSILON = 1e-06
ROPE_BASE = 1000000.0
MASK_VALUE = -1e30
SCORE_SCALE = 1.0 / HEAD_DIM**0.5

FEAT = D // N_TP
SHARD = FEAT // N_REP
LANES = 128
HALF_TP = N_TP // 2
N_X = 4
PART = FEAT // N_X
SLOTS = 8
USED = GROUP + 2
BLOCK = KV_HEADS * SLOTS
PER_CORE = KV_HEADS // 2
HALF_ROWS = PER_CORE * SLOTS
SUMS = HALF_ROWS + SLOTS
DESTS = N_X * HALF_TP
WIDE = 3 * LANES

f32 = jnp.float32
bf16 = jnp.bfloat16
MIB = 1 << 20

VMEM = pl.BlockSpec(memory_space=pltpu.VMEM)
SMEM = pl.BlockSpec(memory_space=pltpu.SMEM)
ANY = pl.BlockSpec(memory_space=pl.ANY)


def params(mib, grid=False):
    kwargs = dict(dimension_semantics=("arbitrary",) * grid) if grid else {}
    return pltpu.CompilerParams(vmem_limit_bytes=int(mib * MIB), **kwargs)

def gather_kernel(ids_ref, tail_ref, table_ref, out_ref, buf, cols, found, places, sems):
    window = table_ref.shape[1]
    tail_start = window // LANES * LANES
    start = lax.axis_index("rep") * window

    count = jnp.int32(0)
    for i in range(TOKENS):
        step = ((i >> 5) & 1) * 2 + (i & 1)
        row = ((i >> 3) & 3) * 8 + (i >> 6) * 4 + ((i >> 1) & 3)
        local = ids_ref[step, row] - start
        found[count] = i
        places[count] = local
        count = count + ((local >= 0) & (local < window)).astype(jnp.int32)

    def copy(j, local):
        base = pl.multiple_of((local >> 7) << 7, LANES)
        return pltpu.make_async_copy(
            table_ref.at[:, pl.ds(base, LANES)], buf.at[j], sems.at[j]
        )

    def begin(j, carry):
        local = places[j]

        @pl.when(local < tail_start)
        def _():
            copy(j, local).start()

        return carry

    lax.fori_loop(0, count, begin, 0)
    cols[...] = jnp.zeros_like(cols)
    lane = lax.broadcasted_iota(jnp.int32, (FEAT, LANES), 1)

    def place(i, local, block):
        shift = (i - local) & (LANES - 1)
        moved = pltpu.roll(block.astype(f32), shift, 1)
        cols[:FEAT] = jnp.where(lane == i, moved, cols[:FEAT])

    def end(j, carry):
        i, local = found[j], places[j]

        @pl.when(local < tail_start)
        def _():
            copy(j, local).wait()
            place(i, local, buf[j])

        @pl.when(local >= tail_start)
        def _():
            place(i, local, tail_ref[...])

        return carry

    lax.fori_loop(0, count, end, 0)
    rows = cols[...].T
    for zh in range(2):
        early = rows[zh * 64 : zh * 64 + DESTS]
        late = rows[zh * 64 + DESTS : zh * 64 + 2 * DESTS]
        tiles = [early[:, n * LANES : (n + 1) * LANES] for n in range(WIDE // LANES)]
        for xx in range(N_X):
            part = late[:, xx * PART : (xx + 1) * PART]
            blank = jnp.zeros((DESTS, LANES - PART), f32)
            block = jnp.concatenate(tiles + [jnp.concatenate([part, blank], axis=1)], axis=0)
            out_ref[xx * 2 + zh] = block.astype(bf16)


def gather_rows(token_ids, embed_table):
    table = embed_table.T
    tail = table.shape[1] // LANES
    return pl.pallas_call(
        gather_kernel,
        grid=(1,),
        in_specs=[SMEM, pl.BlockSpec((FEAT, LANES), lambda i: (0, tail)), ANY],
        out_specs=VMEM,
        out_shape=jax.ShapeDtypeStruct((N_REP, 4 * DESTS, LANES), bf16),
        scratch_shapes=[
            pltpu.VMEM((TOKENS, FEAT, LANES), bf16),
            pltpu.VMEM((WIDE, LANES), f32),
            pltpu.SMEM((TOKENS,), jnp.int32),
            pltpu.SMEM((TOKENS,), jnp.int32),
            pltpu.SemaphoreType.DMA((TOKENS,)),
        ],
        compiler_params=params(55),
        name="gather_rows",
    )(token_ids.T, table, table)


def old_columns_kernel(old_ref, out_ref, sems):
    xx = lax.axis_index("rep") >> 1
    copies = []
    for n, (first, width, to) in enumerate(
        (
            (0, 2 * GROUP, 0),
            (HEADS, 2, 2 * GROUP),
            (HEADS + KV_HEADS, 2, 2 * GROUP + 2),
        )
    ):
        at = pl.multiple_of((first + xx * width) * HEAD_DIM, HEAD_DIM)
        copies.append(
            pltpu.make_async_copy(
                old_ref.at[:, pl.ds(at, width * HEAD_DIM)],
                out_ref.at[:, pl.ds(to * HEAD_DIM, width * HEAD_DIM)],
                sems.at[n],
            )
        )
        copies[-1].start()
    for copy in copies:
        copy.wait()


def take_old_columns(old_qkv):
    shape = (FEAT, 2 * USED * HEAD_DIM)
    return pl.pallas_call(
        old_columns_kernel,
        in_specs=[ANY],
        out_specs=VMEM,
        out_shape=jax.ShapeDtypeStruct(shape, bf16),
        scratch_shapes=[pltpu.SemaphoreType.DMA((3,))],
        compiler_params=params(8),
        cost_estimate=pl.CostEstimate(
            flops=0, bytes_accessed=4 * shape[0] * shape[1], transcendentals=0
        ),
        name="take_old_columns",
    )(old_qkv)


def project_kernel(x_ref, gain_ref, new_ref, other_ref, old, keep_ref, send_ref):
    rep, core = lax.axis_index("rep"), lax.axis_index("tp") & 1
    xx, zh = rep >> 1, rep & 1
    embedded = jnp.sum(x_ref[...].astype(f32), axis=0)
    early = jnp.concatenate(
        [embedded[n * DESTS : (n + 1) * DESTS] for n in range(WIDE // LANES)], axis=1
    )
    late = embedded[3 * DESTS :]
    squares = [
        jnp.broadcast_to(jnp.sum(e * e, axis=1, keepdims=True), (DESTS, LANES))
        for e in (late, early)
    ]
    gain = gain_ref[...].astype(f32)
    part_gain = jnp.zeros((1, PART), f32)
    for i in range(N_X):
        part_gain = part_gain + jnp.where(xx == i, gain[:, i * PART : (i + 1) * PART], 0.0)
    early = (early[:, :FEAT] * gain).astype(bf16)
    late = (late[:, :PART] * part_gain).astype(bf16)
    first, second = late[:, :SHARD], late[:, SHARD:]
    late_own = jnp.where(zh == 0, first, second)
    late_other = jnp.where(zh == 0, second, first)

    def put(out_ref, group, slot, value):
        out_ref[pl.ds(group * SLOTS + slot, DESTS, stride=SUMS), :] = value

    for out_ref, side in ((keep_ref, core), (send_ref, 1 - core)):
        for j in range(PER_CORE):
            head = j * 2 + side
            starts = (
                (head * (GROUP * HEAD_DIM), GROUP, 0),
                (HEADS * HEAD_DIM + head * HEAD_DIM, 1, GROUP),
                ((HEADS + KV_HEADS) * HEAD_DIM + head * HEAD_DIM, 1, GROUP + 1),
            )
            for start, width, slot in starts:
                columns = pl.ds(pl.multiple_of(start, HEAD_DIM), width * HEAD_DIM)
                sums = jnp.dot(
                    late_own, new_ref[:, columns], preferred_element_type=f32
                ) + jnp.dot(late_other, other_ref[:, columns], preferred_element_type=f32)
                for g in range(width):
                    put(out_ref, j, slot + g, sums[:, g * HEAD_DIM : (g + 1) * HEAD_DIM])
            put(out_ref, j, SLOTS - 1, squares[0])
    sums = jnp.dot(early, old[...], preferred_element_type=f32)
    for slot in range(USED):
        at = (slot, slot + GROUP) if slot < GROUP else (slot * 2, slot * 2 + 1)
        both = [sums[:, a * HEAD_DIM : (a + 1) * HEAD_DIM] for a in at]
        put(keep_ref, PER_CORE, slot, jnp.where(core == 0, both[0], both[1]))
        put(send_ref, PER_CORE, slot, jnp.where(core == 0, both[1], both[0]))
    for out_ref in (keep_ref, send_ref):
        put(out_ref, PER_CORE, SLOTS - 1, squares[1])


def project(received, norm_gain, new_qkv, other_qkv, old_columns):
    out = jax.ShapeDtypeStruct((DESTS * SUMS, LANES), f32)
    return pl.pallas_call(
        project_kernel,
        in_specs=[VMEM] * 5,
        out_specs=[VMEM, VMEM],
        out_shape=[out, out],
        compiler_params=params(16),
        name="project",
    )(received, norm_gain.reshape(1, FEAT), new_qkv, other_qkv, old_columns)


def add_kernel(a_ref, b_ref, out_ref):
    out_ref[...] = a_ref[...] + b_ref[...]


def add(a, b):
    return pl.pallas_call(
        add_kernel,
        in_specs=[VMEM, VMEM],
        out_specs=VMEM,
        out_shape=jax.ShapeDtypeStruct(a.shape, a.dtype),
        compiler_params=params(16),
        name="add",
    )(a, b)


def finish_kernel(x_ref, cos_ref, sin_ref, *refs):
    out_ref = refs[-1]
    parts = x_ref[...].reshape(N_X, HALF_TP, SUMS, LANES)
    late = jnp.sum(jnp.sum(parts[:, :, :HALF_ROWS], axis=1), axis=0)
    early = jnp.sum(parts[:, :, HALF_ROWS:], axis=1)
    summed = jnp.concatenate([early.reshape(HALF_ROWS, LANES), late], axis=0).reshape(
        2, PER_CORE, SLOTS, LANES
    )
    squares = summed[:, :, SLOTS - 1 :, :]
    normed = summed / jnp.sqrt(squares / D + NORM_EPSILON)
    swapped = pltpu.roll(normed.reshape(BLOCK, LANES), HEAD_DIM // 2, 1).reshape(normed.shape)
    rotated = normed * cos_ref[...].reshape(2, 1, 1, LANES) + swapped * sin_ref[...].reshape(
        2, 1, 1, LANES
    )
    slot = lax.broadcasted_iota(jnp.int32, normed.shape, 2)
    result = jnp.where(slot <= GROUP, rotated, jnp.where(slot == GROUP + 1, normed, 0.0))
    out_ref[...] = jnp.broadcast_to(
        result.reshape(1, BLOCK, LANES).astype(bf16), out_ref.shape
    )


def finish(received, cosine, sine, *far):
    return pl.pallas_call(
        finish_kernel,
        in_specs=[VMEM, VMEM, VMEM] + [ANY] * len(far),
        out_specs=VMEM,
        out_shape=jax.ShapeDtypeStruct((N_TP, BLOCK, LANES), bf16),
        compiler_params=params(52),
        name="finish",
    )(received, cosine, sine, *far)


def attend_kernel(len_ref, q_ref, kv_ref, out_ref, scores_ref, weights_ref):
    row = pl.program_id(0)
    tp = lax.axis_index("tp")
    chunk = kv_ref.shape[1]
    value_at = KV_HEADS * HEAD_DIM
    count = STEPS * SLOTS
    blocks = [(row * 2 + s % 2) * 2 for s in range(STEPS)]
    rows_of = [slice(s // 2 * HALF_ROWS, (s // 2 + 1) * HALF_ROWS) for s in range(STEPS)]
    contract_last = (((1,), (1,)), ((), ()))
    by_core = [
        jnp.stack(
            [
                q_ref[b + core, r].astype(f32).reshape(PER_CORE, SLOTS, LANES)
                for b, r in zip(blocks, rows_of)
            ],
            axis=1,
        )
        for core in range(2)
    ]
    wide = jnp.stack(by_core, axis=1).reshape(KV_HEADS, count, LANES)
    queries = [wide[h].astype(bf16) for h in range(KV_HEADS)]
    shifted = [pltpu.roll(wide[h], count - 1, 0).astype(bf16) for h in range(KV_HEADS)]
    new = []
    for h in range(KV_HEADS):
        columns = slice(h * HEAD_DIM, (h + 1) * HEAD_DIM)
        scores_ref[h * count : (h + 1) * count, :] = lax.dot_general(
            queries[h], kv_ref[row, :, columns], contract_last, preferred_element_type=f32
        )
        new.append(
            lax.dot_general(queries[h], queries[h], contract_last, preferred_element_type=f32)
        )
    valid = len_ref[row] - tp * chunk
    shape = scores_ref.shape
    position = lax.broadcasted_iota(jnp.int32, shape, 1)
    scores = jnp.where(position < valid, scores_ref[...] * SCORE_SCALE, MASK_VALUE)
    from_step = (lax.broadcasted_iota(jnp.int32, (shape[0], count), 0) >> 3) & (STEPS - 1)
    column = lax.broadcasted_iota(jnp.int32, (shape[0], count), 1)
    new_mask = ((column & (SLOTS - 1)) == GROUP) & ((column >> 3) <= from_step) & (tp == 0)
    scores_new = jnp.where(new_mask, jnp.concatenate(new, axis=0) * SCORE_SCALE, MASK_VALUE)
    peak = jnp.maximum(
        jnp.max(scores, axis=1, keepdims=True), jnp.max(scores_new, axis=1, keepdims=True)
    )
    weights = jnp.exp(scores - peak).astype(bf16)
    weights_new = jnp.exp(scores_new - peak).astype(bf16)
    weights_ref[...] = weights
    total = jnp.sum(weights.astype(f32), axis=1, keepdims=True) + jnp.sum(
        weights_new.astype(f32), axis=1, keepdims=True
    )
    numerator = []
    for h in range(0, KV_HEADS, 2):
        columns = slice(value_at + h * HEAD_DIM, value_at + (h + 2) * HEAD_DIM)
        rows = slice(h * count, (h + 2) * count)
        both = jnp.dot(weights_ref[rows, :], kv_ref[row, :, columns], preferred_element_type=f32)
        for n in range(2):
            at = slice((h + n) * count, (h + n + 1) * count)
            numerator.append(
                both[n * count : (n + 1) * count, n * LANES : (n + 1) * LANES]
                + jnp.dot(weights_new[at], shifted[h + n], preferred_element_type=f32)
            )
    grouped = (KV_HEADS, STEPS, SLOTS, LANES)
    part = (jnp.concatenate(numerator, axis=0) / total).reshape(grouped)
    slot = lax.broadcasted_iota(jnp.int32, grouped, 2)
    diagonal = slot == lax.broadcasted_iota(jnp.int32, grouped, 3)
    log_total = jnp.broadcast_to(peak + jnp.log(total), (shape[0], LANES)).reshape(grouped)
    log_row = jnp.sum(jnp.where(diagonal, log_total, 0.0), axis=2, keepdims=True)
    high = log_row.astype(bf16).astype(f32)
    middle = (log_row - high).astype(bf16).astype(f32)
    low = log_row - high - middle
    part = jnp.where(
        slot < GROUP,
        part,
        jnp.where(slot == GROUP, high, jnp.where(slot == GROUP + 1, middle, low)),
    )
    by_core = part.reshape(PER_CORE, 2, STEPS, SLOTS, LANES)
    for core in range(2):
        for s, (b, r) in enumerate(zip(blocks, rows_of)):
            out_ref[b + core, r] = by_core[:, core, s].reshape(HALF_ROWS, LANES).astype(bf16)


def attend(cache_len, gathered, kv_cache):
    chunk = kv_cache.shape[1]
    whole = pl.BlockSpec((N_TP, BLOCK, LANES), lambda r: (0, 0, 0))
    lines = KV_HEADS * STEPS * SLOTS
    return pl.pallas_call(
        attend_kernel,
        grid=(ROWS,),
        in_specs=[
            SMEM,
            whole,
            VMEM,
        ],
        out_specs=whole,
        out_shape=jax.ShapeDtypeStruct((N_TP, BLOCK, LANES), bf16),
        scratch_shapes=[pltpu.VMEM((lines, chunk), f32), pltpu.VMEM((lines, chunk), bf16)],
        compiler_params=params(16, 1),
        name="attend",
    )(cache_len, gathered, kv_cache)


def merge_kernel(x_ref, out_ref):
    x = x_ref[...].astype(f32).reshape(N_TP, KV_HEADS, SLOTS, LANES)
    log_row = jnp.sum(x[:, :, GROUP:, :], axis=2, keepdims=True)
    slot = lax.broadcasted_iota(jnp.int32, x.shape, 2)
    lane = lax.broadcasted_iota(jnp.int32, x.shape, 3)
    log_total = jnp.sum(jnp.where(slot == lane, log_row, 0.0), axis=3, keepdims=True)
    share = jnp.exp(log_total - jnp.max(log_total, axis=0, keepdims=True))
    heads = jnp.sum(share * x, axis=0) / jnp.sum(share, axis=0)
    packed = jnp.concatenate([heads[h, :GROUP] for h in range(KV_HEADS)], axis=0)
    out_ref[...] = jnp.broadcast_to(packed.astype(bf16)[None], out_ref.shape)


def merge(received):
    return pl.pallas_call(
        merge_kernel,
        in_specs=[VMEM],
        out_specs=VMEM,
        out_shape=jax.ShapeDtypeStruct((N_TP, HEADS, LANES), bf16),
        compiler_params=params(16),
        name="merge",
    )(received)


def output_kernel(*refs):
    x_ref, old_ref, *pieces, out_ref, wide, heads, late_parts = refs
    rep = lax.axis_index("rep")
    xx, zh = rep >> 1, rep & 1
    wide[...] = x_ref[...].astype(f32).reshape(wide.shape)
    for h in range(HEADS):
        kv = h // GROUP
        at = kv % 2 * HEADS + kv // 2 * GROUP + h % GROUP
        rows = [
            wide[pl.ds(at + el * HEADS // 2, HALF_TP, stride=2 * HEADS), :] for el in range(2)
        ]
        heads[:, h * HEAD_DIM : (h + 1) * HEAD_DIM] = jnp.concatenate(rows, axis=0).astype(bf16)
    contract_last = (((1,), (1,)), ((), ()))
    early_heads, late_heads = heads[:HALF_TP], heads[HALF_TP:]
    for n, piece in enumerate(pieces):
        place = ((xx + n // 2) & (N_X - 1)) * 2 + (zh ^ (n & 1))
        late_parts[place, :, :SHARD] = lax.dot_general(
            late_heads, piece[...], contract_last, preferred_element_type=f32
        )
    early = lax.dot_general(
        early_heads, old_ref[...], contract_last, preferred_element_type=f32
    )
    late = jnp.concatenate([late_parts[r, :, :SHARD] for r in range(N_REP)], axis=1)
    for r in range(ROWS):
        for el, total in enumerate((early, late)):
            out_ref[r, el * 2 : el * 2 + 2, :] = total[r * 2 : r * 2 + 2, :].astype(bf16)


def output(gathered, old_out, pieces):
    return pl.pallas_call(
        output_kernel,
        in_specs=[VMEM] * (2 + N_REP),
        out_specs=VMEM,
        out_shape=jax.ShapeDtypeStruct((ROWS, STEPS, FEAT), bf16),
        scratch_shapes=[
            pltpu.VMEM((N_TP * HEADS, LANES), f32),
            pltpu.VMEM((N_TP, D), bf16),
            pltpu.VMEM((N_REP, HALF_TP, LANES), f32),
        ],
        compiler_params=params(16),
        name="output",
    )(gathered, old_out.T, *pieces)


def rotation(cache_len):
    tp = lax.axis_index("tp")
    half_dim = HEAD_DIM // 2
    inverse_freq = ROPE_BASE ** (-jnp.arange(half_dim, dtype=f32) * 2.0 / HEAD_DIM)
    positions = cache_len[tp >> 2] + ((tp >> 1) & 1) + 2 * jnp.arange(2, dtype=jnp.int32)
    angles = positions.astype(f32)[:, None] * inverse_freq[None, :]
    cosine, sine = jnp.cos(angles), jnp.sin(angles)
    return (
        jnp.concatenate([cosine, cosine], axis=1),
        jnp.concatenate([-sine, sine], axis=1),
    )


def body(
    token_ids, cache_len, embed_table, norm_gain, old_qkv, old_out, new_qkv, new_out, kv_cache
):
    turn = [(r, r ^ 1) for r in range(N_REP)]
    ahead = [(r, (r + 2) % N_REP) for r in range(N_REP)]
    back = [(r, (r - 2) % N_REP) for r in range(N_REP)]
    other_qkv = lax.ppermute(new_qkv, "rep", turn)
    cosine, sine = rotation(cache_len)
    rows = gather_rows(token_ids, embed_table)
    rows, old_qkv = lax.optimization_barrier((rows, old_qkv))
    old_columns = take_old_columns(old_qkv)
    rows = lax.all_to_all(rows, "rep", 0, 0)
    rows, old_columns, cosine, sine = lax.optimization_barrier((rows, old_columns, cosine, sine))
    keep, send = project(rows, norm_gain, new_qkv, other_qkv, old_columns)
    arrived = lax.ppermute(send, "tp", [(t, t ^ 1) for t in range(N_TP)])
    summed = add(keep, arrived).reshape(DESTS, SUMS, LANES)
    groups = [
        [(x * 2 + zh) * N_TP + k * 2 + core for x in range(N_X) for k in range(HALF_TP)]
        for zh in range(2)
        for core in range(2)
    ]
    partials = lax.all_to_all(summed, ("rep", "tp"), 0, 0, axis_index_groups=groups)
    partials, own = lax.optimization_barrier((partials, new_out.T))
    other = lax.ppermute(own, "rep", turn)
    behind_own = lax.ppermute(own, "rep", ahead)
    front_own = lax.ppermute(own, "rep", back)
    projected = lax.all_to_all(finish(partials, cosine, sine, embed_table.T, embed_table.T, old_qkv), "tp", 0, 0)
    projected, other, behind_own, front_own = lax.optimization_barrier(
        (projected, other, behind_own, front_own)
    )
    far_own = lax.ppermute(behind_own, "rep", ahead)
    front_other = lax.ppermute(other, "rep", back)
    parts = lax.all_to_all(attend(cache_len, projected, kv_cache), "tp", 0, 0)
    parts, front_other, other, far_own = lax.optimization_barrier(
        (parts, front_other, other, far_own)
    )
    far_other = lax.ppermute(front_other, "rep", back)
    behind_other = lax.ppermute(other, "rep", ahead)
    heads = lax.all_to_all(merge(parts), "tp", 0, 0)
    pieces = (
        own,
        other,
        front_own,
        front_other,
        far_own,
        far_other,
        behind_own,
        behind_other,
    )
    return output(heads, old_out, pieces)


def solution(mesh):
    in_specs = (
        P(),
        P("rep"),
        P("rep", "tp"),
        P("tp"),
        P("tp", None),
        P(None, "tp"),
        P(("tp", "rep"), None),
        P(None, ("tp", "rep")),
        P("rep", "tp", None),
    )
    out_specs = P("rep", None, "tp")
    return jax.shard_map(body, mesh=mesh, in_specs=in_specs, out_specs=out_specs, check_vma=False)
```

```python
import functools

import jax
import jax.numpy as jnp
from jax import lax
from jax.experimental import pallas as pl
from jax.experimental.pallas import tpu as pltpu
from jax.sharding import PartitionSpec as P

D = 5120
HEADS = 40
KV_HEADS = 8
HEAD_DIM = 128
GROUP = HEADS // KV_HEADS
STEPS = 4
OLD_STEPS = 2
ROWS = 4
N_REP = 8
N_TP = 16
TOKENS = N_REP * ROWS * STEPS

NORM_EPSILON = 1e-06
ROPE_BASE = 1000000.0
MASK_VALUE = -1e30
SCORE_SCALE = 1.0 / HEAD_DIM**0.5

FEAT = D // N_TP
SHARD = FEAT // N_REP
LANES = 128
HALF_TP = N_TP // 2
N_X = 4
PART = FEAT // N_X
SLOTS = 8
USED = GROUP + 2
BLOCK = KV_HEADS * SLOTS
PER_CORE = KV_HEADS // 2
HALF_ROWS = PER_CORE * SLOTS
SUMS = HALF_ROWS + SLOTS
DESTS = N_X * HALF_TP
WIDE = 3 * LANES

f32 = jnp.float32
bf16 = jnp.bfloat16
MIB = 1 << 20

VMEM = pl.BlockSpec(memory_space=pltpu.VMEM)
SMEM = pl.BlockSpec(memory_space=pltpu.SMEM)
ANY = pl.BlockSpec(memory_space=pl.ANY)


def params(mib, grid=False):
    kwargs = dict(dimension_semantics=("arbitrary",) * grid) if grid else {}
    return pltpu.CompilerParams(vmem_limit_bytes=int(mib * MIB), **kwargs)

def gather_kernel(ids_ref, tail_ref, table_ref, out_ref, buf, cols, found, places, sems):
    window = table_ref.shape[1]
    tail_start = window // LANES * LANES
    start = lax.axis_index("rep") * window

    count = jnp.int32(0)
    for i in range(TOKENS):
        step = ((i >> 5) & 1) * 2 + (i & 1)
        row = ((i >> 3) & 3) * 8 + (i >> 6) * 4 + ((i >> 1) & 3)
        local = ids_ref[step, row] - start
        found[count] = i
        places[count] = local
        count = count + ((local >= 0) & (local < window)).astype(jnp.int32)

    def copy(j, local):
        base = pl.multiple_of((local >> 7) << 7, LANES)
        return pltpu.make_async_copy(
            table_ref.at[:, pl.ds(base, LANES)], buf.at[j], sems.at[j]
        )

    def begin(j, carry):
        local = places[j]

        @pl.when(local < tail_start)
        def _():
            copy(j, local).start()

        return carry

    lax.fori_loop(0, count, begin, 0)
    cols[...] = jnp.zeros_like(cols)
    lane = lax.broadcasted_iota(jnp.int32, (FEAT, LANES), 1)

    def place(i, local, block):
        shift = (i - local) & (LANES - 1)
        moved = pltpu.roll(block.astype(f32), shift, 1)
        cols[:FEAT] = jnp.where(lane == i, moved, cols[:FEAT])

    def end(j, carry):
        i, local = found[j], places[j]

        @pl.when(local < tail_start)
        def _():
            copy(j, local).wait()
            place(i, local, buf[j])

        @pl.when(local >= tail_start)
        def _():
            place(i, local, tail_ref[...])

        return carry

    lax.fori_loop(0, count, end, 0)
    rows = cols[...].T
    for zh in range(2):
        early = rows[zh * 64 : zh * 64 + DESTS]
        late = rows[zh * 64 + DESTS : zh * 64 + 2 * DESTS]
        tiles = [early[:, n * LANES : (n + 1) * LANES] for n in range(WIDE // LANES)]
        for xx in range(N_X):
            part = late[:, xx * PART : (xx + 1) * PART]
            blank = jnp.zeros((DESTS, LANES - PART), f32)
            block = jnp.concatenate(tiles + [jnp.concatenate([part, blank], axis=1)], axis=0)
            out_ref[xx * 2 + zh] = block.astype(bf16)


def gather_rows(token_ids, embed_table):
    table = embed_table.T
    tail = table.shape[1] // LANES
    return pl.pallas_call(
        gather_kernel,
        grid=(1,),
        in_specs=[SMEM, pl.BlockSpec((FEAT, LANES), lambda i: (0, tail)), ANY],
        out_specs=VMEM,
        out_shape=jax.ShapeDtypeStruct((N_REP, 4 * DESTS, LANES), bf16),
        scratch_shapes=[
            pltpu.VMEM((TOKENS, FEAT, LANES), bf16),
            pltpu.VMEM((WIDE, LANES), f32),
            pltpu.SMEM((TOKENS,), jnp.int32),
            pltpu.SMEM((TOKENS,), jnp.int32),
            pltpu.SemaphoreType.DMA((TOKENS,)),
        ],
        compiler_params=params(55),
        name="gather_rows",
    )(token_ids.T, table, table)


def old_columns_kernel(old_ref, out_ref, sems):
    xx = lax.axis_index("rep") >> 1
    copies = []
    for n, (first, width, to) in enumerate(
        (
            (0, 2 * GROUP, 0),
            (HEADS, 2, 2 * GROUP),
            (HEADS + KV_HEADS, 2, 2 * GROUP + 2),
        )
    ):
        at = pl.multiple_of((first + xx * width) * HEAD_DIM, HEAD_DIM)
        copies.append(
            pltpu.make_async_copy(
                old_ref.at[:, pl.ds(at, width * HEAD_DIM)],
                out_ref.at[:, pl.ds(to * HEAD_DIM, width * HEAD_DIM)],
                sems.at[n],
            )
        )
        copies[-1].start()
    for copy in copies:
        copy.wait()


def take_old_columns(old_qkv):
    shape = (FEAT, 2 * USED * HEAD_DIM)
    return pl.pallas_call(
        old_columns_kernel,
        in_specs=[ANY],
        out_specs=VMEM,
        out_shape=jax.ShapeDtypeStruct(shape, bf16),
        scratch_shapes=[pltpu.SemaphoreType.DMA((3,))],
        compiler_params=params(8),
        cost_estimate=pl.CostEstimate(
            flops=0, bytes_accessed=4 * shape[0] * shape[1], transcendentals=0
        ),
        name="take_old_columns",
    )(old_qkv)


def project_kernel(own, x_ref, gain_ref, new_ref, other_ref, old, out_ref):
    rep, core = lax.axis_index("rep"), lax.axis_index("tp") & 1
    xx, zh = rep >> 1, rep & 1
    embedded = jnp.sum(x_ref[...].astype(f32), axis=0)
    early = jnp.concatenate(
        [embedded[n * DESTS : (n + 1) * DESTS] for n in range(WIDE // LANES)], axis=1
    )
    late = embedded[3 * DESTS :]
    squares = [
        jnp.broadcast_to(jnp.sum(e * e, axis=1, keepdims=True), (DESTS, LANES))
        for e in (late, early)
    ]
    gain = gain_ref[...].astype(f32)
    part_gain = jnp.zeros((1, PART), f32)
    for i in range(N_X):
        part_gain = part_gain + jnp.where(xx == i, gain[:, i * PART : (i + 1) * PART], 0.0)
    early = (early[:, :FEAT] * gain).astype(bf16)
    late = (late[:, :PART] * part_gain).astype(bf16)
    first, second = late[:, :SHARD], late[:, SHARD:]
    late_own = jnp.where(zh == 0, first, second)
    late_other = jnp.where(zh == 0, second, first)

    def put(out_ref, group, slot, value):
        out_ref[pl.ds(group * SLOTS + slot, DESTS, stride=SUMS), :] = value

    for side in (core if own else 1 - core,):
        for j in range(PER_CORE):
            head = j * 2 + side
            starts = (
                (head * (GROUP * HEAD_DIM), GROUP, 0),
                (HEADS * HEAD_DIM + head * HEAD_DIM, 1, GROUP),
                ((HEADS + KV_HEADS) * HEAD_DIM + head * HEAD_DIM, 1, GROUP + 1),
            )
            for start, width, slot in starts:
                columns = pl.ds(pl.multiple_of(start, HEAD_DIM), width * HEAD_DIM)
                sums = jnp.dot(
                    late_own, new_ref[:, columns], preferred_element_type=f32
                ) + jnp.dot(late_other, other_ref[:, columns], preferred_element_type=f32)
                for g in range(width):
                    put(out_ref, j, slot + g, sums[:, g * HEAD_DIM : (g + 1) * HEAD_DIM])
            put(out_ref, j, SLOTS - 1, squares[0])
    sums = jnp.dot(early, old[...], preferred_element_type=f32)
    for slot in range(USED):
        at = (slot, slot + GROUP) if slot < GROUP else (slot * 2, slot * 2 + 1)
        both = [sums[:, a * HEAD_DIM : (a + 1) * HEAD_DIM] for a in at]
        put(out_ref, PER_CORE, slot, jnp.where(core == (0 if own else 1), both[0], both[1]))
    put(out_ref, PER_CORE, SLOTS - 1, squares[1])


def project(own, received, norm_gain, new_qkv, other_qkv, old_columns):
    return pl.pallas_call(
        functools.partial(project_kernel, own),
        in_specs=[VMEM] * 5,
        out_specs=VMEM,
        out_shape=jax.ShapeDtypeStruct((DESTS * SUMS, LANES), f32),
        compiler_params=params(16),
        cost_estimate=pl.CostEstimate(flops=0, bytes_accessed=4 * MIB, transcendentals=0),
        name="project",
    )(received, norm_gain.reshape(1, FEAT), new_qkv, other_qkv, old_columns)


def add_kernel(a_ref, b_ref, out_ref):
    out_ref[...] = a_ref[...] + b_ref[...]


def add(a, b):
    return pl.pallas_call(
        add_kernel,
        in_specs=[VMEM, VMEM],
        out_specs=VMEM,
        out_shape=jax.ShapeDtypeStruct(a.shape, a.dtype),
        compiler_params=params(16),
        name="add",
    )(a, b)


def finish_kernel(x_ref, cos_ref, sin_ref, *refs):
    out_ref = refs[-1]
    parts = x_ref[...].reshape(N_X, HALF_TP, SUMS, LANES)
    late = jnp.sum(jnp.sum(parts[:, :, :HALF_ROWS], axis=1), axis=0)
    early = jnp.sum(parts[:, :, HALF_ROWS:], axis=1)
    summed = jnp.concatenate([early.reshape(HALF_ROWS, LANES), late], axis=0).reshape(
        2, PER_CORE, SLOTS, LANES
    )
    squares = summed[:, :, SLOTS - 1 :, :]
    normed = summed / jnp.sqrt(squares / D + NORM_EPSILON)
    swapped = pltpu.roll(normed.reshape(BLOCK, LANES), HEAD_DIM // 2, 1).reshape(normed.shape)
    rotated = normed * cos_ref[...].reshape(2, 1, 1, LANES) + swapped * sin_ref[...].reshape(
        2, 1, 1, LANES
    )
    slot = lax.broadcasted_iota(jnp.int32, normed.shape, 2)
    result = jnp.where(slot <= GROUP, rotated, jnp.where(slot == GROUP + 1, normed, 0.0))
    out_ref[...] = jnp.broadcast_to(
        result.reshape(1, BLOCK, LANES).astype(bf16), out_ref.shape
    )


def finish(received, cosine, sine, *far):
    return pl.pallas_call(
        finish_kernel,
        in_specs=[VMEM, VMEM, VMEM] + [ANY] * len(far),
        out_specs=VMEM,
        out_shape=jax.ShapeDtypeStruct((N_TP, BLOCK, LANES), bf16),
        compiler_params=params(52),
        name="finish",
    )(received, cosine, sine, *far)


def attend_kernel(len_ref, q_ref, kv_ref, out_ref, scores_ref, weights_ref):
    row = pl.program_id(0)
    tp = lax.axis_index("tp")
    chunk = kv_ref.shape[1]
    value_at = KV_HEADS * HEAD_DIM
    count = STEPS * SLOTS
    blocks = [(row * 2 + s % 2) * 2 for s in range(STEPS)]
    rows_of = [slice(s // 2 * HALF_ROWS, (s // 2 + 1) * HALF_ROWS) for s in range(STEPS)]
    contract_last = (((1,), (1,)), ((), ()))
    by_core = [
        jnp.stack(
            [
                q_ref[b + core, r].astype(f32).reshape(PER_CORE, SLOTS, LANES)
                for b, r in zip(blocks, rows_of)
            ],
            axis=1,
        )
        for core in range(2)
    ]
    wide = jnp.stack(by_core, axis=1).reshape(KV_HEADS, count, LANES)
    queries = [wide[h].astype(bf16) for h in range(KV_HEADS)]
    shifted = [pltpu.roll(wide[h], count - 1, 0).astype(bf16) for h in range(KV_HEADS)]
    new = []
    for h in range(KV_HEADS):
        columns = slice(h * HEAD_DIM, (h + 1) * HEAD_DIM)
        scores_ref[h * count : (h + 1) * count, :] = lax.dot_general(
            queries[h], kv_ref[row, :, columns], contract_last, preferred_element_type=f32
        )
        new.append(
            lax.dot_general(queries[h], queries[h], contract_last, preferred_element_type=f32)
        )
    valid = len_ref[row] - tp * chunk
    shape = scores_ref.shape
    position = lax.broadcasted_iota(jnp.int32, shape, 1)
    scores = jnp.where(position < valid, scores_ref[...] * SCORE_SCALE, MASK_VALUE)
    from_step = (lax.broadcasted_iota(jnp.int32, (shape[0], count), 0) >> 3) & (STEPS - 1)
    column = lax.broadcasted_iota(jnp.int32, (shape[0], count), 1)
    new_mask = ((column & (SLOTS - 1)) == GROUP) & ((column >> 3) <= from_step) & (tp == 0)
    scores_new = jnp.where(new_mask, jnp.concatenate(new, axis=0) * SCORE_SCALE, MASK_VALUE)
    peak = jnp.maximum(
        jnp.max(scores, axis=1, keepdims=True), jnp.max(scores_new, axis=1, keepdims=True)
    )
    weights = jnp.exp(scores - peak).astype(bf16)
    weights_new = jnp.exp(scores_new - peak).astype(bf16)
    weights_ref[...] = weights
    total = jnp.sum(weights.astype(f32), axis=1, keepdims=True) + jnp.sum(
        weights_new.astype(f32), axis=1, keepdims=True
    )
    numerator = []
    for h in range(0, KV_HEADS, 2):
        columns = slice(value_at + h * HEAD_DIM, value_at + (h + 2) * HEAD_DIM)
        rows = slice(h * count, (h + 2) * count)
        both = jnp.dot(weights_ref[rows, :], kv_ref[row, :, columns], preferred_element_type=f32)
        for n in range(2):
            at = slice((h + n) * count, (h + n + 1) * count)
            numerator.append(
                both[n * count : (n + 1) * count, n * LANES : (n + 1) * LANES]
                + jnp.dot(weights_new[at], shifted[h + n], preferred_element_type=f32)
            )
    grouped = (KV_HEADS, STEPS, SLOTS, LANES)
    part = (jnp.concatenate(numerator, axis=0) / total).reshape(grouped)
    slot = lax.broadcasted_iota(jnp.int32, grouped, 2)
    diagonal = slot == lax.broadcasted_iota(jnp.int32, grouped, 3)
    log_total = jnp.broadcast_to(peak + jnp.log(total), (shape[0], LANES)).reshape(grouped)
    log_row = jnp.sum(jnp.where(diagonal, log_total, 0.0), axis=2, keepdims=True)
    high = log_row.astype(bf16).astype(f32)
    middle = (log_row - high).astype(bf16).astype(f32)
    low = log_row - high - middle
    part = jnp.where(
        slot < GROUP,
        part,
        jnp.where(slot == GROUP, high, jnp.where(slot == GROUP + 1, middle, low)),
    )
    by_core = part.reshape(PER_CORE, 2, STEPS, SLOTS, LANES)
    for core in range(2):
        for s, (b, r) in enumerate(zip(blocks, rows_of)):
            out_ref[b + core, r] = by_core[:, core, s].reshape(HALF_ROWS, LANES).astype(bf16)


def attend(cache_len, gathered, kv_cache):
    chunk = kv_cache.shape[1]
    whole = pl.BlockSpec((N_TP, BLOCK, LANES), lambda r: (0, 0, 0))
    lines = KV_HEADS * STEPS * SLOTS
    return pl.pallas_call(
        attend_kernel,
        grid=(ROWS,),
        in_specs=[
            SMEM,
            whole,
            VMEM,
        ],
        out_specs=whole,
        out_shape=jax.ShapeDtypeStruct((N_TP, BLOCK, LANES), bf16),
        scratch_shapes=[pltpu.VMEM((lines, chunk), f32), pltpu.VMEM((lines, chunk), bf16)],
        compiler_params=params(16, 1),
        name="attend",
    )(cache_len, gathered, kv_cache)


def merge_kernel(x_ref, out_ref):
    x = x_ref[...].astype(f32).reshape(N_TP, KV_HEADS, SLOTS, LANES)
    log_row = jnp.sum(x[:, :, GROUP:, :], axis=2, keepdims=True)
    slot = lax.broadcasted_iota(jnp.int32, x.shape, 2)
    lane = lax.broadcasted_iota(jnp.int32, x.shape, 3)
    log_total = jnp.sum(jnp.where(slot == lane, log_row, 0.0), axis=3, keepdims=True)
    share = jnp.exp(log_total - jnp.max(log_total, axis=0, keepdims=True))
    heads = jnp.sum(share * x, axis=0) / jnp.sum(share, axis=0)
    packed = jnp.concatenate([heads[h, :GROUP] for h in range(KV_HEADS)], axis=0)
    out_ref[...] = jnp.broadcast_to(packed.astype(bf16)[None], out_ref.shape)


def merge(received):
    return pl.pallas_call(
        merge_kernel,
        in_specs=[VMEM],
        out_specs=VMEM,
        out_shape=jax.ShapeDtypeStruct((N_TP, HEADS, LANES), bf16),
        compiler_params=params(16),
        name="merge",
    )(received)


def output_kernel(*refs):
    x_ref, old_ref, *pieces, out_ref, wide, heads, late_parts = refs
    rep = lax.axis_index("rep")
    xx, zh = rep >> 1, rep & 1
    wide[...] = x_ref[...].astype(f32).reshape(wide.shape)
    for h in range(HEADS):
        kv = h // GROUP
        at = kv % 2 * HEADS + kv // 2 * GROUP + h % GROUP
        rows = [
            wide[pl.ds(at + el * HEADS // 2, HALF_TP, stride=2 * HEADS), :] for el in range(2)
        ]
        heads[:, h * HEAD_DIM : (h + 1) * HEAD_DIM] = jnp.concatenate(rows, axis=0).astype(bf16)
    contract_last = (((1,), (1,)), ((), ()))
    early_heads, late_heads = heads[:HALF_TP], heads[HALF_TP:]
    for n, piece in enumerate(pieces):
        place = ((xx + n // 2) & (N_X - 1)) * 2 + (zh ^ (n & 1))
        late_parts[place, :, :SHARD] = lax.dot_general(
            late_heads, piece[...], contract_last, preferred_element_type=f32
        )
    early = lax.dot_general(
        early_heads, old_ref[...], contract_last, preferred_element_type=f32
    )
    late = jnp.concatenate([late_parts[r, :, :SHARD] for r in range(N_REP)], axis=1)
    for r in range(ROWS):
        for el, total in enumerate((early, late)):
            out_ref[r, el * 2 : el * 2 + 2, :] = total[r * 2 : r * 2 + 2, :].astype(bf16)


def output(gathered, old_out, pieces):
    return pl.pallas_call(
        output_kernel,
        in_specs=[VMEM] * (2 + N_REP),
        out_specs=VMEM,
        out_shape=jax.ShapeDtypeStruct((ROWS, STEPS, FEAT), bf16),
        scratch_shapes=[
            pltpu.VMEM((N_TP * HEADS, LANES), f32),
            pltpu.VMEM((N_TP, D), bf16),
            pltpu.VMEM((N_REP, HALF_TP, LANES), f32),
        ],
        compiler_params=params(16),
        name="output",
    )(gathered, old_out.T, *pieces)


def rotation(cache_len):
    tp = lax.axis_index("tp")
    half_dim = HEAD_DIM // 2
    inverse_freq = ROPE_BASE ** (-jnp.arange(half_dim, dtype=f32) * 2.0 / HEAD_DIM)
    positions = cache_len[tp >> 2] + ((tp >> 1) & 1) + 2 * jnp.arange(2, dtype=jnp.int32)
    angles = positions.astype(f32)[:, None] * inverse_freq[None, :]
    cosine, sine = jnp.cos(angles), jnp.sin(angles)
    return (
        jnp.concatenate([cosine, cosine], axis=1),
        jnp.concatenate([-sine, sine], axis=1),
    )


def body(
    token_ids, cache_len, embed_table, norm_gain, old_qkv, old_out, new_qkv, new_out, kv_cache
):
    turn = [(r, r ^ 1) for r in range(N_REP)]
    ahead = [(r, (r + 2) % N_REP) for r in range(N_REP)]
    back = [(r, (r - 2) % N_REP) for r in range(N_REP)]
    other_qkv = lax.ppermute(new_qkv, "rep", turn)
    cosine, sine = rotation(cache_len)
    rows = gather_rows(token_ids, embed_table)
    rows, old_qkv = lax.optimization_barrier((rows, old_qkv))
    old_columns = take_old_columns(old_qkv)
    rows = lax.all_to_all(rows, "rep", 0, 0)
    rows, old_columns, cosine, sine = lax.optimization_barrier((rows, old_columns, cosine, sine))
    send, keep = (
        project(own, rows, norm_gain, new_qkv, other_qkv, old_columns) for own in (False, True)
    )
    arrived = lax.ppermute(send, "tp", [(t, t ^ 1) for t in range(N_TP)])
    summed = add(keep, arrived).reshape(DESTS, SUMS, LANES)
    groups = [
        [(x * 2 + zh) * N_TP + k * 2 + core for x in range(N_X) for k in range(HALF_TP)]
        for zh in range(2)
        for core in range(2)
    ]
    partials = lax.all_to_all(summed, ("rep", "tp"), 0, 0, axis_index_groups=groups)
    partials, own = lax.optimization_barrier((partials, new_out.T))
    other = lax.ppermute(own, "rep", turn)
    behind_own = lax.ppermute(own, "rep", ahead)
    front_own = lax.ppermute(own, "rep", back)
    projected = lax.all_to_all(finish(partials, cosine, sine, embed_table.T, embed_table.T, old_qkv), "tp", 0, 0)
    projected, other, behind_own, front_own = lax.optimization_barrier(
        (projected, other, behind_own, front_own)
    )
    far_own = lax.ppermute(behind_own, "rep", ahead)
    front_other = lax.ppermute(other, "rep", back)
    parts = lax.all_to_all(attend(cache_len, projected, kv_cache), "tp", 0, 0)
    parts, front_other, other, far_own = lax.optimization_barrier(
        (parts, front_other, other, far_own)
    )
    far_other = lax.ppermute(front_other, "rep", back)
    behind_other = lax.ppermute(other, "rep", ahead)
    heads = lax.all_to_all(merge(parts), "tp", 0, 0)
    pieces = (
        own,
        other,
        front_own,
        front_other,
        far_own,
        far_other,
        behind_own,
        behind_other,
    )
    return output(heads, old_out, pieces)


def solution(mesh):
    in_specs = (
        P(),
        P("rep"),
        P("rep", "tp"),
        P("tp"),
        P("tp", None),
        P(None, "tp"),
        P(("tp", "rep"), None),
        P(None, ("tp", "rep")),
        P("rep", "tp", None),
    )
    out_specs = P("rep", None, "tp")
    return jax.shard_map(body, mesh=mesh, in_specs=in_specs, out_specs=out_specs, check_vma=False)
```
